128 devices in a mesh: gx: 8 (over x, core), gy: 16 (over y, z).
Axes of the slice: x: 4, y: 4, z: 4, core: 2. Of those that a mesh axis runs over, the one named last changes fastest.
Arguments:
- tracers: float32 [2, 30, 768, 1024], P(None, None, 'gy', 'gx'), may hold values from -6 to 6
- east_flow: float32 [30, 768, 1024], P(None, 'gy', 'gx'), may hold values from -0.15 to 0.15
- north_flow: float32 [30, 768, 1024], P(None, 'gy', 'gx'), may hold values from -0.15 to 0.15
- ocean_kappa: float32 [29, 768, 1024], P(None, 'gy', 'gx'), may hold values from 0.05 to 5
- land_sea: int32 [768, 1024], P('gy', 'gx'), may hold values 0 or 1
- air_temp: float32 [16, 256, 1024], P(None, 'gy', 'gx'), may hold values from -6 to 6
- air_kappa: float32 [16, 256, 1024], P(None, 'gy', 'gx'), may hold values from 0.05 to 5
- air_fluxes: float32 [4, 256, 1024], P(None, 'gy', 'gx'), may hold values from -6 to 6
- weight_tiles: float32 [128, 64, 1024], P(('gx', 'gy'))
- tile_index: int32 [128, 128, 16], P(('gx', 'gy')), may hold values from 0 to 63
- send_blocks: int32 [128, 128, 16], P(('gx', 'gy')), may hold values from 0 to 192, as said below
- receive_blocks: int32 [128, 128, 16], P(('gx', 'gy')), may hold values from 0 to 64, as said below
Outputs:
- tracers_next: float32 [2, 30, 768, 1024], P(None, None, 'gy', 'gx')
- air_temp_next: float32 [16, 256, 1024], P(None, 'gy', 'gx')
- surface_fields: float32 [4, 256, 1024], P(None, 'gy', 'gx')
The draws below stay inside these ranges and needn't reach their ends.
Inputs may be any that keep to these rules, and one draw needn't show every extreme that they name: For each pair of devices the live slots come first along the last dimension; slot k of send_blocks[s, r] is live exactly when slot k of receive_blocks[r, s] is; 192 marks an empty slot. Every pair has at least one live slot, and some device has all 16 slots live from every device. `receive_blocks`: 64 marks an empty slot.
All inputs are finite; a program needn't handle non-finite values. No bound on the sum of `land_sea` on one device may be relied on, other than what follows from the above.
Results may differ from the reference program's by a relative error of at most 0.0003.
Values sent between devices are 32-bit elements; how exact they have to be, the bound alone decides.
A program may use at most 192 MiB of HBM per device.

```python
import math
import jax
import jax.numpy as jnp
from jax import lax

OX = 128
OY = 48
AX = 128
AY = 16
LO = 30
LA = 16
NT = 2
NF = 4
B = 32
CAP = 16
TILES = 64
ADV = 4
NY = 768
NX = 1024
NAY = 256
NAX = 1024
OB = 192
AB = 64
N_GX = 8
N_GY = 16
DEVICES = 128


def pair_counts(key):
    key_counts, key_busiest = jax.random.split(key)
    device_total = N_GX * N_GY
    counts = jax.random.randint(key_counts, (device_total, device_total), 1, CAP + 1)
    busiest = jax.random.randint(key_busiest, (), 0, device_total)
    column = jnp.arange(device_total)[None, :]
    return jnp.where(column == busiest, CAP, counts)


def draw_send_blocks(key, part):
    counts = pair_counts(key)
    key = jax.random.fold_in(key, 3)
    device_total = N_GX * N_GY
    blocks = jax.random.randint(key, (device_total, device_total, CAP), 0, OB)
    slot_index = jnp.arange(CAP)[None, None, :]
    return jnp.where(slot_index < counts[:, :, None], blocks, OB).astype(jnp.int32)


def draw_receive_blocks(key, part):
    counts = pair_counts(key).T
    key = jax.random.fold_in(key, 4)
    device_total = N_GX * N_GY
    blocks = jax.random.randint(key, (device_total, device_total, CAP), 0, AB)
    slot_index = jnp.arange(CAP)[None, None, :]
    return jnp.where(slot_index < counts[:, :, None], blocks, AB).astype(jnp.int32)


def draw_weight_tiles(key, part):
    key = jax.random.fold_in(key, 5)
    key_diag, key_off = jax.random.split(key)
    device_total = N_GX * N_GY
    diagonal = jax.random.uniform(key_diag, (device_total, TILES, B), jnp.float32, 0.5, 1.0)
    spread = 0.26 * jax.random.normal(key_off, (device_total, TILES, B, B), jnp.float32)
    identity = jnp.eye(B, dtype=jnp.float32)
    tiles = (spread / math.sqrt(B) * (1.0 - identity) + diagonal[..., :, None] * identity) / 8.0
    return tiles.reshape(device_total, TILES, B * B).astype(jnp.float32)


def place_ends(values, stream_key, least, largest):
    spot = [jax.random.randint(jax.random.fold_in(stream_key, axis), (), 0, length) for axis, length in enumerate(values.shape)]
    widest = values.shape.index(max(values.shape))
    neighbour = spot[:widest] + [(spot[widest] + 1) % values.shape[widest]] + spot[widest + 1:]
    return values.at[tuple(spot)].set(least).at[tuple(neighbour)].set(largest)


def steps_of(own_key, dims, shards, smallest, largest):
    level, own = 1.0, jax.random.fold_in(own_key, 6)
    for dim, shards_of in shards:
        heights = jnp.exp(jax.random.uniform(jax.random.fold_in(own, dim), (shards_of,), jnp.float32, smallest / len(shards), largest / len(shards)))
        level = level * jnp.repeat(heights, dims[dim] // shards_of).reshape([-1 if axis == dim else 1 for axis in range(len(dims))])
    return level


def gaussian(key, extent, scale, reach, cuts=(), kind=jnp.bfloat16):
    values = scale * jax.random.normal(key, extent, jnp.float32)
    if cuts:
        values = values * steps_of(key, extent, cuts, -0.22, 0.18)
    return jnp.clip(values, -reach, reach).astype(kind)


def setup_inputs(seed: int = 0) -> dict:
    splits = jax.random.split(jax.random.key(seed), 13)
    return {
        "tracers": gaussian(splits[0], (NT, LO, NY, NX), 1.0, 6.0, ((2, 16), (3, 8)), jnp.float32),
        "east_flow": jnp.clip(jax.random.uniform(splits[1], (LO, NY, NX), jnp.float32, -0.15, 0.15) * steps_of(splits[1], (LO, NY, NX), ((1, 16), (2, 8)), -0.4, 0.0), -0.15, 0.15),
        "north_flow": jnp.clip(jax.random.uniform(splits[2], (LO, NY, NX), jnp.float32, -0.15, 0.15) * steps_of(splits[2], (LO, NY, NX), ((1, 16), (2, 8)), -0.4, 0.0), -0.15, 0.15),
        "ocean_kappa": jnp.clip(jnp.exp(math.log(5.0) - 4.6051702 * jax.random.uniform(splits[3], (LO - 1, NY, NX), jnp.float32) ** steps_of(splits[3], (LO - 1, NY, NX), ((1, 16), (2, 8)), -0.2, 0.2)), 0.05, 5.0),
        "land_sea": place_ends((jax.random.randint(splits[4], (NY, NX), 0, 10) < 7).astype(jnp.int32), jax.random.fold_in(splits[4], 1), 0, 1),
        "air_temp": gaussian(splits[5], (LA, NAY, NAX), 1.0, 6.0, ((1, 16), (2, 8)), jnp.float32),
        "air_kappa": jnp.clip(jnp.exp(math.log(5.0) - 4.6051702 * jax.random.uniform(splits[6], (LA, NAY, NAX), jnp.float32) ** steps_of(splits[6], (LA, NAY, NAX), ((1, 16), (2, 8)), -0.2, 0.2)), 0.05, 5.0),
        "air_fluxes": gaussian(splits[7], (NF, NAY, NAX), 1.0, 6.0, ((1, 16), (2, 8)), jnp.float32),
        "weight_tiles": draw_weight_tiles(jax.random.fold_in(splits[12], 71), 0),
        "tile_index": place_ends(jax.random.randint(splits[9], (DEVICES, DEVICES, CAP), 0, TILES), jax.random.fold_in(splits[9], 1), 0, TILES - 1).astype(jnp.int32),
        "send_blocks": draw_send_blocks(jax.random.fold_in(splits[12], 71), 0),
        "receive_blocks": draw_receive_blocks(jax.random.fold_in(splits[12], 71), 0),
    }


def transport(values, across, along, flow_east, flow_north, open_east, open_north):
    east_vel = flow_east[..., :-1]
    face_east = (open_east[:, :-1] * open_east[:, 1:]) * (jnp.maximum(east_vel, 0.0) * across[..., :-1] + jnp.minimum(east_vel, 0.0) * across[..., 1:])
    north_vel = flow_north[..., :-1, :]
    face_north = (open_north[:-1, :] * open_north[1:, :]) * (jnp.maximum(north_vel, 0.0) * along[..., :-1, :] + jnp.minimum(north_vel, 0.0) * along[..., 1:, :])
    return values - (face_east[..., 1:] - face_east[..., :-1]) - (face_north[..., 1:, :] - face_north[..., :-1, :])


def thomas(below_coef, diag_coef, above_coef, source_terms):
    ratio_list = [above_coef[0] / diag_coef[0]]
    value_list = [source_terms[0] / diag_coef[0]]
    for layer_index in range(1, len(diag_coef)):
        pivot_value = diag_coef[layer_index] - below_coef[layer_index] * ratio_list[-1]
        ratio_list.append(above_coef[layer_index] / pivot_value)
        value_list.append((source_terms[layer_index] - below_coef[layer_index] * value_list[-1]) / pivot_value)
    result = [value_list[-1]]
    for layer_index in range(len(diag_coef) - 2, -1, -1):
        result.append(value_list[layer_index] - ratio_list[layer_index] * result[-1])
    return result[::-1]


def ocean_mix(advected, ocean_kappa, sea, forcing):
    layers = advected.shape[1]
    links = [ocean_kappa[layer_index] * sea for layer_index in range(layers - 1)]
    flat_zero = jnp.zeros_like(sea)
    below_coef = [flat_zero] + [-link_value for link_value in links]
    above_coef = [-link_value for link_value in links] + [flat_zero]
    diag_coef = [1.0 - below_coef[layer_index] - above_coef[layer_index] for layer_index in range(layers)]
    sources = [advected[:, layer_index] for layer_index in range(layers)]
    sources[0] = sources[0] + forcing
    return jnp.stack(thomas(below_coef, diag_coef, above_coef, sources), axis=1)


def air_mix(air_temp, air_kappa, ground):
    layers = air_temp.shape[0]
    flat_zero = jnp.zeros_like(ground)
    below_coef = [flat_zero] + [-air_kappa[layer_index] for layer_index in range(1, layers)]
    above_coef = [-air_kappa[layer_index + 1] for layer_index in range(layers - 1)] + [flat_zero]
    diag_coef = [1.0 + air_kappa[0] - above_coef[0]] + [1.0 - below_coef[layer_index] - above_coef[layer_index] for layer_index in range(1, layers)]
    sources = [air_temp[0] + air_kappa[0] * ground] + [air_temp[layer_index] for layer_index in range(1, layers)]
    return jnp.stack(thomas(below_coef, diag_coef, above_coef, sources), axis=0)


def device_blocks(fields, rows_here, cols_here):
    field_count = fields.shape[0]
    shaped = fields.reshape(field_count, N_GY, rows_here, N_GX, cols_here // B, B)
    shaped = shaped.transpose(3, 1, 2, 4, 0, 5)
    return shaped.reshape(N_GX * N_GY, rows_here * (cols_here // B), field_count * B)


def device_fields(blocks, rows_here, cols_here, field_count):
    shaped = blocks.reshape(N_GX, N_GY, rows_here, cols_here // B, field_count, B)
    shaped = shaped.transpose(4, 1, 2, 0, 3, 5)
    return shaped.reshape(field_count, N_GY * rows_here, N_GX * cols_here)


def reference(tracers, east_flow, north_flow, ocean_kappa, land_sea, air_temp, air_kappa, air_fluxes, weight_tiles, tile_index, send_blocks, receive_blocks):
    device_count = N_GX * N_GY
    sea = land_sea.astype(jnp.float32)
    sources = jnp.arange(device_count, dtype=jnp.int32)
    owners = sources[:, None]
    air_blocks = device_blocks(air_fluxes, AY, AX)

    def pull_one(source):
        targets = receive_blocks[:, source, :]
        live = targets < AB
        picked = air_blocks[owners, jnp.minimum(targets, AB - 1)]
        picked = jnp.where(live[:, :, None], picked, 0.0).reshape(device_count, CAP, NF, B)
        tiles = weight_tiles[source][tile_index[source]].reshape(device_count, CAP, B, B)
        spread = jnp.einsum("rkab,rkfa->rkfb", tiles, picked, precision=lax.Precision.HIGHEST)
        empty = jnp.zeros((OB, NF * B), jnp.float32)
        return empty.at[send_blocks[source]].add(spread.reshape(device_count, CAP, NF * B), mode="drop")

    ocean_blocks = lax.map(pull_one, sources)
    forcing_fields = device_fields(ocean_blocks, OY, OX, NF)

    flow_east = jnp.concatenate([east_flow[..., -1:], east_flow, east_flow[..., :1]], axis=-1)
    flow_north = jnp.concatenate([jnp.zeros_like(north_flow[..., :1, :]), north_flow, north_flow[..., -1:, :]], axis=-2)
    open_east = jnp.concatenate([sea[:, -1:], sea, sea[:, :1]], axis=1)
    open_north = jnp.concatenate([jnp.zeros_like(sea[:1, :]), sea, sea[-1:, ::-1]], axis=0)
    values = tracers
    for step_index in range(ADV):
        across = jnp.concatenate([values[..., -1:], values, values[..., :1]], axis=-1)
        along = jnp.concatenate([jnp.zeros_like(values[..., :1, :]), values, values[..., -1:, ::-1]], axis=-2)
        values = transport(values, across, along, flow_east, flow_north, open_east, open_north)
    forcing = jnp.stack([sea * forcing_fields[0], sea * forcing_fields[1]], axis=0)
    tracers_next = ocean_mix(values, ocean_kappa, sea, forcing)

    surface = jnp.stack([sea * tracers_next[0, 0], sea, sea * (east_flow[0] + 0.1 * jnp.tanh(forcing_fields[2])), sea * (north_flow[0] + 0.1 * jnp.tanh(forcing_fields[3]))], axis=0)
    surface_blocks = device_blocks(surface, OY, OX)

    def push_one(total, source):
        chosen = send_blocks[source]
        live = chosen < OB
        picked = surface_blocks[source][jnp.minimum(chosen, OB - 1)].reshape(device_count, CAP, NF, B)
        tiles = weight_tiles[source][tile_index[source]].reshape(device_count, CAP, B, B)
        mapped = jnp.einsum("rkab,rkfb->rkfa", tiles, picked, precision=lax.Precision.HIGHEST)
        mapped = jnp.where(live[:, :, None, None], mapped, 0.0).reshape(device_count, CAP, NF * B)
        total = total.at[owners, receive_blocks[:, source, :]].add(mapped, mode="drop")
        return total, None

    start_total = jnp.zeros((device_count, AB, NF * B), jnp.float32)
    air_blocks_in = lax.scan(push_one, start_total, sources)[0]
    surface_fields = device_fields(air_blocks_in, AY, AX, NF)
    ground = air_temp[0] * (1.0 - surface_fields[1]) + surface_fields[0]
    air_temp_next = air_mix(air_temp, air_kappa, ground)
    return tracers_next, air_temp_next, surface_fields
```

```python
import jax
import jax.numpy as jnp
from jax import lax
from jax.experimental import pallas as pl
from jax.experimental.pallas import tpu as pltpu
from jax.sharding import PartitionSpec as P

F32 = jnp.float32
BF16 = jnp.bfloat16
MESH = pl.DeviceIdType.MESH
NF, B, CAP, ADV = 4, 32, 16, 4
GX, GY = 8, 16
DEV = GX * GY
SLOTS = DEV * CAP
LO, LA, OY, AY, LN = 30, 16, 48, 16, 128
PL = 2 * LO
TOP = 8
CHUNKS, CW = 8, 256
STRIDE = 37


def iota(shape, dim):
    return lax.broadcasted_iota(jnp.int32, shape, dim)


def split(x):
    hi = x.astype(BF16)
    return hi, (x - hi.astype(F32)).astype(BF16)


def fields_to_blocks(fields, q):
    lane = iota(fields[0].shape, 1) >> 5
    out = jnp.zeros_like(fields[0])
    for f in range(NF):
        moved = pltpu.roll(fields[f], ((f - q) * B) % LN, 1) if f != q else fields[f]
        out = jnp.where(lane == f, moved, out)
    return out


def blocks_to_field(groups, f):
    lane = iota(groups[0].shape, 1) >> 5
    out = jnp.zeros_like(groups[0])
    for q in range(4):
        moved = pltpu.roll(groups[q], ((q - f) * B) % LN, 1) if f != q else groups[q]
        out = jnp.where(lane == q, moved, out)
    return out


def slot_rows(idx):
    spread = (iota((CAP, LN), 1) & (CAP - 1)) == iota((CAP, LN), 0)
    tiled = jnp.dot(idx.astype(F32).astype(BF16), spread.astype(F32).astype(BF16), preferred_element_type=F32)
    own = (iota((DEV, LN), 1) >> 4) == (iota((DEV, LN), 0) & 7)
    return jnp.sum(jnp.where(own, tiled, 0.0).reshape(16, 8, LN), axis=1)


def kernel(
    tr, ue, un, kap, land, atemp, akap, aflux, wts, tix, sbl, rbl,
    out_tr, out_air, out_sf,
    v, u, n, kv, land_v, sea_p, at_v, ak_v, af_v, w_v, ti_v, sb_v, rb_v,
    rows3, w2t, w2p, oh_t, oh_h, oh_b, g1, g2,
    send1, recv1, send2, recv2, xt, sp, st,
    rsend, rrecv, csend, crecv,
    c0, ce, cw, cn, cs, elim_r, elim_z, top_y, air_r, air_z, x_out,
    in_sem, out_sem, hs_sem, hr_sem, a_sem,
):
    gx = lax.axis_index("gx")
    gy = lax.axis_index("gy")
    me = gx * GY + gy

    pairs = (
        (aflux, af_v), (rbl.at[0], rb_v), (land, land_v), (tr, v.at[0, :, TOP:TOP + OY, :]), (ue, u), (un, n),
        (wts.at[0], w_v), (tix.at[0], ti_v), (sbl.at[0], sb_v), (kap, kv), (atemp, at_v), (akap, ak_v),
    )
    loads = [pltpu.make_async_copy(s, d, in_sem.at[i]) for i, (s, d) in enumerate(pairs)]
    for c in loads:
        c.start()

    barrier = pltpu.get_barrier_semaphore()

    def peer(i):
        o = lax.rem(i * STRIDE, DEV)
        px = lax.rem(gx + lax.div(o, 16), GX)
        yz = lax.rem(o, 16)
        py = lax.rem(lax.div(gy, 4) + lax.div(yz, 4), 4) * 4 + lax.rem(lax.rem(gy, 4) + lax.rem(yz, 4), 4)
        return px, py

    def greet(i, carry):
        px, py = peer(i)
        pl.semaphore_signal(barrier, inc=1, device_id=(px, py), device_id_type=MESH)
        return carry

    lax.fori_loop(1, DEV, greet, 0)

    lane48 = iota((OY, LN), 1)
    row48 = iota((OY, LN), 0)

    loads[0].wait()
    loads[1].wait()
    tgt = rb_v[...]
    tgt = jnp.where(tgt < 64, (tgt & 3) * AY + (tgt >> 2), -1)
    rows3[1] = slot_rows(tgt)
    air = [af_v[f] for f in range(NF)]
    blocks = jnp.concatenate([fields_to_blocks(air, q) for q in range(4)], axis=0)
    bhi, blo = split(blocks)
    blocks2 = jnp.concatenate([bhi, blo], axis=0)
    sub128 = iota((LN, LN), 0)

    def pick(g, carry):
        row = rows3[1, pl.ds(g, 1), :]
        hot = jnp.where((sub128 & 63).astype(F32) == row, 1.0, 0.0)
        oh_b[g] = hot[:64].astype(BF16)
        picked = jnp.dot(hot.T.astype(BF16), blocks2, preferred_element_type=F32)
        send1[pl.ds(g * 8, 8)] = picked.reshape(8, CAP, LN)
        return carry

    lax.fori_loop(0, 16, pick, 0)

    for i in (2, 3, 4, 5):
        loads[i].wait()
    sea = land_v[...].astype(F32)
    sea_p[TOP:TOP + OY, :] = sea

    def first_edges(l, carry):
        acc, accu = carry
        for t in range(2):
            p = t * LO + l
            x = v[0, p, TOP:TOP + OY, :]
            acc = jnp.where((lane48 >> 1) == p, pltpu.roll(x, 2 * p + 1, 1), acc)
            rsend[0, 0, pl.ds(p, 1), :] = x[OY - 1:OY]
            rsend[0, 1, pl.ds(p, 1), :] = x[0:1]
        accu = jnp.where(lane48 == l, pltpu.roll(u[l] * sea, l + 1, 1), accu)
        rsend[0, 0, pl.ds(PL + l, 1), :] = n[l, OY - 1:OY, :] * sea[OY - 1:OY]
        return acc, accu

    zero48 = jnp.zeros((OY, LN), F32)
    acc, accu = lax.fori_loop(0, LO, first_edges, (zero48, zero48))
    acc = jnp.where((lane48 >> 1) == PL, pltpu.roll(sea, 2 * PL + 1, 1), acc)
    csend[0, 0] = acc
    csend[0, 1] = accu
    rsend[0, 1, PL:96, :] = jnp.zeros((96 - PL, LN), F32)
    tail = jnp.where(iota((8, LN), 0) == 2, sea[OY - 1:OY], 0.0)
    rsend[0, 0, 88:96, :] = jnp.where(iota((8, LN), 0) < 2, rsend[0, 0, 88:96, :], tail)
    rsend[0, 1, 88:96, :] = jnp.where(iota((8, LN), 0) == 2, sea[0:1], 0.0)

    @pl.when(gy == 0)
    def _():
        for s in range(ADV):
            rrecv[s, 1] = jnp.zeros((96, LN), F32)

    pl.semaphore_wait(barrier, DEV - 1)

    east, west = lax.rem(gx + 1, GX), lax.rem(gx + GX - 1, GX)

    def lines(s):
        return 96 if s == 0 else 64

    def sides(s):
        return 2 if s == 0 else 1

    def row_copy(s, out, into, to):
        return pltpu.make_async_remote_copy(
            src_ref=rsend.at[s, out, 0:lines(s), :], dst_ref=rrecv.at[s, into, 0:lines(s), :],
            send_sem=hs_sem.at[s, out], recv_sem=hr_sem.at[s, into], device_id=to, device_id_type=MESH)

    def col_copy(s, out, into, to):
        return pltpu.make_async_remote_copy(
            src_ref=csend.at[s, 0:sides(s)], dst_ref=crecv.at[s, into, 0:sides(s)],
            send_sem=hs_sem.at[s, 2 + out], recv_sem=hr_sem.at[s, 2 + into], device_id=to, device_id_type=MESH)

    def send_edges(s):
        col_copy(s, 0, 0, (east, gy)).start()
        col_copy(s, 1, 1, (west, gy)).start()

        @pl.when(gy < GY - 1)
        def _():
            row_copy(s, 0, 1, (gx, gy + 1)).start()

        @pl.when(gy == GY - 1)
        def _():
            row_copy(s, 0, 0, (GX - 1 - gx, gy)).start()

        @pl.when(gy > 0)
        def _():
            row_copy(s, 1, 0, (gx, gy - 1)).start()

    flip = jnp.where(iota((LN, LN), 0) + iota((LN, LN), 1) == LN - 1, 1.0, 0.0)

    def await_edges(s):
        col_copy(s, 0, 0, (east, gy)).wait()
        col_copy(s, 1, 1, (west, gy)).wait()
        row_copy(s, 0, 0, (east, gy)).wait()

        @pl.when(gy > 0)
        def _():
            row_copy(s, 1, 1, (east, gy)).wait()

        @pl.when(gy == GY - 1)
        def _():
            rows = rrecv[s, 0, 0:lines(s), :]
            rrecv[s, 0, 0:lines(s), :] = jnp.dot(
                rows, flip, precision=lax.Precision.HIGHEST, preferred_element_type=F32)

    send_edges(0)

    def exchange_out(i, carry):
        px, py = peer(i)
        pltpu.make_async_remote_copy(
            src_ref=send1.at[px * GY + py], dst_ref=recv1.at[me], send_sem=a_sem.at[0], recv_sem=a_sem.at[1],
            device_id=(px, py), device_id_type=MESH).start()
        return carry

    lax.fori_loop(1, DEV, exchange_out, 0)
    recv1[me] = send1[me]

    for i in (6, 7, 8):
        loads[i].wait()
    rows3[0] = slot_rows(ti_v[...])
    snd = sb_v[...]
    rows3[2] = slot_rows(jnp.where(snd < 192, (snd & 3) * OY + (snd >> 2), -1))
    for c in range(8):
        whi, wlo = split(w_v[:, c * LN:(c + 1) * LN])
        both = jnp.concatenate([whi.astype(F32), wlo.astype(F32)], axis=0)
        w2t[0, c * LN:(c + 1) * LN, :] = both.T
    for b in range(B):
        w2t[1, b * B:(b + 1) * B, :] = w2t[0, pl.ds(b, B, stride=B), :]
    w2p[0] = w2t[0].astype(BF16)
    w2p[1] = w2t[1].astype(BF16)

    def hots(g, carry):
        rt = rows3[0, pl.ds(g, 1), :]
        oh_t[g] = jnp.where((sub128 & 63).astype(F32) == rt, 1.0, 0.0).astype(BF16)
        rs = rows3[2, pl.ds(g, 1), :]
        oh_h[g] = jnp.where(iota((256, LN), 0).astype(F32) == rs, 1.0, 0.0).astype(BF16)
        return carry

    lax.fori_loop(0, 16, hots, 0)

    def tiles(c, carry):
        hot = jnp.concatenate([oh_t[2 * c], oh_t[2 * c + 1]], axis=1)
        g1[c] = jnp.dot(w2p[0], hot, preferred_element_type=F32)
        g2[c] = jnp.dot(w2p[1], hot, preferred_element_type=F32)
        return carry

    lax.fori_loop(0, CHUNKS, tiles, 0)

    await_edges(0)

    def ghosts(s):
        even = (lane48 & 1) == 0
        return jnp.where(even, pltpu.roll(crecv[s, 1, 0], LN - 1, 1), pltpu.roll(crecv[s, 0, 0], 1, 1))

    gh = ghosts(0)
    last = lane48 == LN - 1
    first = lane48 == 0
    gsea = pltpu.roll(gh, LN - 1 - 2 * PL, 1)
    sea_e = jnp.where(last, gsea, pltpu.roll(sea, LN - 1, 1))
    sea_p[TOP + OY:TOP + OY + 1, :] = rrecv[0, 0, 90:91, :]
    sea_n = sea_p[TOP + 1:TOP + 1 + OY, :]
    open_e = sea * sea_e
    open_n = sea * sea_n
    uw_ghost = crecv[0, 0, 1] * jnp.broadcast_to(sea[:, 0:1], (OY, LN))

    def faces(l, carry):
        um = u[l] * open_e
        uw = jnp.where(first, pltpu.roll(uw_ghost, lax.rem(LN - l, LN), 1), pltpu.roll(um, 1, 1))
        nm = n[l] * open_n
        below = rrecv[0, 1, pl.ds(PL + l, 1), :] * sea[0:1]
        ns = jnp.where(row48 == 0, below, pltpu.roll(nm, 1, 0))
        ce[l] = -jnp.minimum(um, 0.0)
        cw[l] = jnp.maximum(uw, 0.0)
        cn[l] = -jnp.minimum(nm, 0.0)
        cs[l] = jnp.maximum(ns, 0.0)
        c0[l] = 1.0 - jnp.maximum(um, 0.0) + jnp.minimum(uw, 0.0) - jnp.maximum(nm, 0.0) + jnp.minimum(ns, 0.0)
        return carry

    lax.fori_loop(0, LO, faces, 0)

    for s in range(ADV):
        if s > 0:
            await_edges(s)
        gh = ghosts(s)
        now, later = s % 2, (s + 1) % 2

        def substep(l, acc, s=s, now=now, later=later, gh=gh):
            k0, ke, kw, kn, ks = c0[l], ce[l], cw[l], cn[l], cs[l]
            for t in range(2):
                p = t * LO + l
                v[now, p, TOP - 1:TOP, :] = rrecv[s, 1, pl.ds(p, 1), :]
                v[now, p, TOP + OY:TOP + OY + 1, :] = rrecv[s, 0, pl.ds(p, 1), :]
                x = v[now, p, TOP:TOP + OY, :]
                g = pltpu.roll(gh, LN - 1 - 2 * p, 1)
                xe = jnp.where(last, g, pltpu.roll(x, LN - 1, 1))
                xw = jnp.where(first, g, pltpu.roll(x, 1, 1))
                y = k0 * x + ke * xe + kw * xw
                y = y + kn * v[now, p, TOP + 1:TOP + 1 + OY, :] + ks * v[now, p, TOP - 1:TOP - 1 + OY, :]
                v[later, p, TOP:TOP + OY, :] = y
                if s < ADV - 1:
                    acc = jnp.where((lane48 >> 1) == p, pltpu.roll(y, 2 * p + 1, 1), acc)
                    rsend[s + 1, 0, pl.ds(p, 1), :] = y[OY - 1:OY]
                    rsend[s + 1, 1, pl.ds(p, 1), :] = y[0:1]
            return acc

        acc = lax.fori_loop(0, LO, substep, zero48)
        if s < ADV - 1:
            csend[s + 1, 0] = acc
            for k in range(2):
                rsend[s + 1, k, PL:64, :] = jnp.zeros((64 - PL, LN), F32)
            send_edges(s + 1)

    loads[9].wait()

    def up(i, carry):
        e, yt, ys = carry
        l = LO - 2 - i
        k = kv[l] * sea
        inv = 1.0 / (e + k)
        r = k * inv
        elim_r[l + 1] = r
        elim_z[0, l + 1] = yt * inv
        elim_z[1, l + 1] = ys * inv
        return (1.0 + k * (1.0 - r), v[0, l, TOP:TOP + OY, :] + r * yt, v[0, LO + l, TOP:TOP + OY, :] + r * ys)

    start = (jnp.ones((OY, LN), F32), v[0, LO - 1, TOP:TOP + OY, :], v[0, PL - 1, TOP:TOP + OY, :])
    e, yt, ys = lax.fori_loop(0, LO - 1, up, start)
    inv = 1.0 / e
    top_y[0], top_y[1], top_y[2] = yt, ys, inv

    loads[10].wait()
    loads[11].wait()

    def air_up(i, carry):
        e, y = carry
        l = LA - 2 - i
        k = ak_v[l + 1]
        inv = 1.0 / (e + k)
        r = k * inv
        air_r[l + 1] = r
        air_z[l + 1] = y * inv
        return 1.0 + k * (1.0 - r), at_v[l] + r * y

    ea, ya = lax.fori_loop(0, LA - 1, air_up, (jnp.ones((AY, LN), F32), at_v[LA - 1]))
    inv_a = 1.0 / (ea + ak_v[0])
    air_z[0] = ya
    air_r[0] = inv_a

    def exchange_wait(snd_buf, rcv_buf, k):
        return pltpu.make_async_remote_copy(
            src_ref=snd_buf.at[pl.ds(0, DEV - 1)], dst_ref=rcv_buf.at[pl.ds(0, DEV - 1)],
            send_sem=a_sem.at[2 * k], recv_sem=a_sem.at[2 * k + 1], device_id=(east, gy), device_id_type=MESH)

    exchange_wait(send1, recv1, 0).wait_recv()

    def apply_tiles(tile_ref, c, h):
        total = jnp.zeros((NF, B, LN), F32)
        for a in range(B):
            w = tile_ref[c, a * B:(a + 1) * B, h * LN:(h + 1) * LN]
            total = total + w[None] * xt[:, a:a + 1, :]
        return total.reshape(NF * B, LN)

    def spread(c, carry):
        for h in range(2):
            xt[...] = recv1[pl.ds(c * 16 + h * 8, 8)].reshape(LN, LN).T.reshape(NF, B, LN)
            hi, lo = split(apply_tiles(g1, c, h))
            sp[2 * c + h, 0:LN, :] = hi
            sp[2 * c + h, LN:, :] = lo
        return carry

    lax.fori_loop(0, CHUNKS, spread, 0)

    def collect(g, total):
        return total + lax.dot_general(
            oh_h[g, 0:192, :], sp[g], (((1,), (1,)), ((), ())), preferred_element_type=F32)

    both = lax.fori_loop(0, 16, collect, jnp.zeros((192, 256), F32))
    landed = both[:, :LN] + both[:, LN:]
    groups = [landed[q * OY:(q + 1) * OY] for q in range(4)]
    force = [blocks_to_field(groups, f) for f in range(NF)]

    xt0 = (top_y[0] + sea * force[0]) * top_y[2]
    xs0 = (top_y[1] + sea * force[1]) * top_y[2]
    surf = [
        sea * xt0,
        sea,
        sea * (u[0] + 0.1 * jnp.tanh(force[2])),
        sea * (n[0] + 0.1 * jnp.tanh(force[3])),
    ]
    sblocks = jnp.concatenate([fields_to_blocks(surf, q) for q in range(4)] + [jnp.zeros((64, LN), F32)], axis=0)
    lifted = jnp.concatenate([sblocks[:LN].T, sblocks[LN:].T], axis=1)
    lhi, llo = split(lifted)
    st[...] = jnp.concatenate([lhi, llo], axis=0)

    def push(i, carry):
        c = lax.rem(gx + 1 + i, GX)
        for h in range(2):
            g = 2 * c + h
            two = jnp.dot(st[...], oh_h[g], preferred_element_type=F32)
            xt[...] = (two[:LN] + two[LN:]).reshape(NF, B, LN)
            send2[pl.ds(g * 8, 8)] = apply_tiles(g2, c, h).T.reshape(8, CAP, LN)

        def out(j, carry2):
            py = lax.rem(gy + j, GY)
            copy = pltpu.make_async_remote_copy(
                src_ref=send2.at[c * GY + py], dst_ref=recv2.at[me], send_sem=a_sem.at[2], recv_sem=a_sem.at[3],
                device_id=(c, py), device_id_type=MESH)
            copy.start()
            return carry2

        @pl.when(i < GX - 1)
        def _():
            lax.fori_loop(0, GY, out, 0)

        @pl.when(i == GX - 1)
        def _():
            lax.fori_loop(1, GY, out, 0)

        return carry

    lax.fori_loop(0, GX, push, 0)
    recv2[me] = send2[me]

    x_out[0] = xt0
    x_out[LO] = xs0

    def down(l, carry):
        a, b = carry
        r = elim_r[l]
        a = elim_z[0, l] + r * a
        b = elim_z[1, l] + r * b
        x_out[l] = a
        x_out[LO + l] = b
        return a, b

    lax.fori_loop(1, LO, down, (xt0, xs0))
    store = pltpu.make_async_copy(x_out, out_tr, out_sem)
    store.start()

    exchange_wait(send2, recv2, 1).wait_recv()

    def gather(g, total):
        hi, lo = split(recv2[pl.ds(g * 8, 8)].reshape(LN, LN))
        return total + jnp.dot(oh_b[g], jnp.concatenate([hi, lo], axis=1), preferred_element_type=F32)

    both = lax.fori_loop(0, 16, gather, jnp.zeros((64, 256), F32))
    landed = both[:, :LN] + both[:, LN:]
    groups = [landed[q * AY:(q + 1) * AY] for q in range(4)]
    fields = [blocks_to_field(groups, f) for f in range(NF)]
    for f in range(NF):
        out_sf[f] = fields[f]
    ground = at_v[0] * (1.0 - fields[1]) + fields[0]
    x = (air_z[0] + ak_v[0] * ground) * air_r[0]
    out_air[0] = x
    for l in range(1, LA):
        x = air_z[l] + air_r[l] * x
        out_air[l] = x

    for s in range(ADV):
        pass
    exchange_wait(send1, recv1, 0).wait_send()
    exchange_wait(send2, recv2, 1).wait_send()
    store.wait()


def shards(
    tracers, east_flow, north_flow, ocean_kappa, land_sea, air_temp, air_kappa, air_fluxes,
    weight_tiles, tile_index, send_blocks, receive_blocks,
):
    anyspace = pl.BlockSpec(memory_space=pl.ANY)
    vm = pl.BlockSpec(memory_space=pltpu.VMEM)
    V = pltpu.VMEM
    scratch = [
        V((2, PL, 64, LN), F32), V((LO, OY, LN), F32), V((LO, OY, LN), F32), V((LO - 1, OY, LN), F32),
        V((OY, LN), jnp.int32), V((64, LN), F32), V((LA, AY, LN), F32), V((LA, AY, LN), F32), V((NF, AY, LN), F32),
        V((64, 1024), F32), V((DEV, CAP), jnp.int32), V((DEV, CAP), jnp.int32), V((DEV, CAP), jnp.int32),
        V((3, 16, LN), F32), V((2, 1024, LN), F32), V((2, 1024, LN), BF16),
        V((16, LN, LN), BF16), V((16, 256, LN), BF16), V((16, 64, LN), BF16),
        V((CHUNKS, 1024, CW), F32), V((CHUNKS, 1024, CW), F32),
        V((DEV, CAP, LN), F32), V((DEV, CAP, LN), F32), V((DEV, CAP, LN), F32), V((DEV, CAP, LN), F32),
        V((NF, B, LN), F32), V((16, 256, LN), BF16), V((256, 256), BF16),
        V((ADV, 2, 96, LN), F32), V((ADV, 2, 96, LN), F32), V((ADV, 2, OY, LN), F32), V((ADV, 2, 2, OY, LN), F32),
        V((LO, OY, LN), F32), V((LO, OY, LN), F32), V((LO, OY, LN), F32), V((LO, OY, LN), F32), V((LO, OY, LN), F32),
        V((LO, OY, LN), F32), V((2, LO, OY, LN), F32), V((3, OY, LN), F32), V((LA, AY, LN), F32), V((LA, AY, LN), F32),
        V((PL, OY, LN), F32),
        pltpu.SemaphoreType.DMA((12,)), pltpu.SemaphoreType.DMA, pltpu.SemaphoreType.DMA((ADV, 4)),
        pltpu.SemaphoreType.DMA((ADV, 4)), pltpu.SemaphoreType.DMA((4,)),
    ]
    out_tr, out_air, out_sf = pl.pallas_call(
        kernel,
        out_shape=(
            jax.ShapeDtypeStruct((PL, OY, LN), F32),
            jax.ShapeDtypeStruct((LA, AY, LN), F32),
            jax.ShapeDtypeStruct((NF, AY, LN), F32),
        ),
        in_specs=[anyspace] * 12,
        out_specs=(anyspace, vm, vm),
        scratch_shapes=scratch,
        compiler_params=pltpu.CompilerParams(
            collective_id=0, has_side_effects=True, vmem_limit_bytes=56 * 1024 * 1024),
        name="coupling_step",
    )(
        tracers.reshape(PL, OY, LN), east_flow, north_flow, ocean_kappa, land_sea, air_temp, air_kappa, air_fluxes,
        weight_tiles, tile_index, send_blocks, receive_blocks,
    )
    return out_tr.reshape(2, LO, OY, LN), out_air, out_sf


def solution(mesh):
    return jax.shard_map(
        shards,
        mesh=mesh,
        in_specs=(
            P(None, None, "gy", "gx"),
            P(None, "gy", "gx"),
            P(None, "gy", "gx"),
            P(None, "gy", "gx"),
            P("gy", "gx"),
            P(None, "gy", "gx"),
            P(None, "gy", "gx"),
            P(None, "gy", "gx"),
            P(("gx", "gy"), None, None),
            P(("gx", "gy"), None, None),
            P(("gx", "gy"), None, None),
            P(("gx", "gy"), None, None),
        ),
        out_specs=(P(None, None, "gy", "gx"), P(None, "gy", "gx"), P(None, "gy", "gx")),
        check_vma=False,
    )
```

```python
import jax
import jax.numpy as jnp
from jax import lax
from jax.experimental import pallas as pl
from jax.experimental.pallas import tpu as pltpu
from jax.sharding import PartitionSpec as P

F32 = jnp.float32
BF16 = jnp.bfloat16
MESH = pl.DeviceIdType.MESH
NF, B, CAP, ADV = 4, 32, 16, 4
GX, GY = 8, 16
DEV = GX * GY
SLOTS = DEV * CAP
LO, LA, OY, AY, LN = 30, 16, 48, 16, 128
PL = 2 * LO
TOP = 8
CHUNKS, CW = 8, 256
GROUP = 5
SENDS = (3, 2, 2, 1)
PARTS = 6


def iota(shape, dim):
    return lax.broadcasted_iota(jnp.int32, shape, dim)


def split(x):
    hi = x.astype(BF16)
    return hi, (x - hi.astype(F32)).astype(BF16)


def fields_to_blocks(fields, q):
    lane = iota(fields[0].shape, 1) >> 5
    out = jnp.zeros_like(fields[0])
    for f in range(NF):
        moved = pltpu.roll(fields[f], ((f - q) * B) % LN, 1) if f != q else fields[f]
        out = jnp.where(lane == f, moved, out)
    return out


def blocks_to_field(groups, f):
    lane = iota(groups[0].shape, 1) >> 5
    out = jnp.zeros_like(groups[0])
    for q in range(4):
        moved = pltpu.roll(groups[q], ((q - f) * B) % LN, 1) if f != q else groups[q]
        out = jnp.where(lane == q, moved, out)
    return out


def slot_rows(idx):
    spread = (iota((CAP, LN), 1) & (CAP - 1)) == iota((CAP, LN), 0)
    tiled = jnp.dot(idx.astype(F32).T.astype(BF16), spread.astype(F32).astype(BF16), preferred_element_type=F32)
    own = (iota((DEV, LN), 1) >> 4) == (iota((DEV, LN), 0) & 7)
    return jnp.sum(jnp.where(own, tiled, 0.0).reshape(16, 8, LN), axis=1)


def kernel(
    tr, ue, un, kap, land, atemp, akap, aflux, wts, tix, sbl, rbl,
    out_tr, out_air, out_sf,
    va, vb, xs, w_shift, w_ghost, w_edge, u, n, kv, land_v, sea_p, at_v, ak_v, af_v, w_v, ti_v, sb_v, rb_v,
    rows3, w2t, w2p, oh_t, oh_h, oh_ht, oh_b, g1, g2,
    send1, recv1, send2, recv2, xt, total, st,
    rsend, rrecv, csend, crecv,
    c0, ce, cw, cn, cs, elim_r, elim_z, top_y, air_r, air_z, x_out,
    in_sem, out_sem, hs_sem, hr_sem, as_sem, ar_sem,
):
    gx = lax.axis_index("gx")
    gy = lax.axis_index("gy")
    me = gx * GY + gy

    pairs = (
        (aflux, af_v), (rbl.at[0], rb_v), (land, land_v), (tr.at[0], va.at[:, 0, TOP:TOP + OY, :]), (ue, u), (un, n),
        (wts.at[0], w_v), (tix.at[0], ti_v), (sbl.at[0], sb_v), (kap, kv), (atemp, at_v), (akap, ak_v),
        (tr.at[1], va.at[:, 1, TOP:TOP + OY, :]),
    )
    loads = [pltpu.make_async_copy(s, d, in_sem.at[i]) for i, (s, d) in enumerate(pairs)]
    for c in loads:
        c.start()

    barrier = pltpu.get_barrier_semaphore()

    def greet(i, carry):
        pl.semaphore_signal(
            barrier, inc=1, device_id=(lax.rem(gx + lax.div(i, GY), GX), lax.rem(gy + lax.rem(i, GY), GY)),
            device_id_type=MESH)
        return carry

    lax.fori_loop(1, DEV, greet, 0)

    lane48 = iota((OY, LN), 1)
    row48 = iota((OY, LN), 0)

    loads[0].wait()
    loads[1].wait()
    tgt = rb_v[...]
    tgt = jnp.where(tgt < 64, (tgt & 3) * AY + (tgt >> 2), -1)
    rows3[1] = slot_rows(tgt)
    air = [af_v[f] for f in range(NF)]
    blocks = jnp.concatenate([fields_to_blocks(air, q) for q in range(4)], axis=0)
    bhi, blo = split(blocks)
    blocks2 = jnp.concatenate([bhi, blo], axis=0)
    sub128 = iota((LN, LN), 0)

    def pick(g, carry):
        row = rows3[1, pl.ds(g, 1), :]
        hot = jnp.where((sub128 & 63).astype(F32) == row, 1.0, 0.0)
        oh_b[g] = hot[:64].astype(BF16)
        picked = jnp.dot(hot.T.astype(BF16), blocks2, preferred_element_type=F32)
        send1[pl.ds(g * 8, 8)] = picked.reshape(8, CAP, LN)
        return carry

    lax.fori_loop(0, 16, pick, 0)

    for i in (2, 3, 4, 5, 12):
        loads[i].wait()
    sea = land_v[...].astype(F32)
    sea_p[TOP:TOP + OY, :] = sea

    src, dst = iota((256, 256), 0) & (LN - 1), iota((256, 256), 1)
    to_east = (src == dst + 1) & (dst < LN - 1)
    to_west = (src == dst - 1 - LN) & (dst > LN)
    w_shift[...] = jnp.where(to_east | to_west, 1.0, 0.0).astype(BF16)
    even = (src & 1) == 0
    w_ghost[...] = jnp.where((even & (dst == LN - 1)) | ((src & 1 == 1) & (dst == LN)), 1.0, 0.0).astype(BF16)
    src, dst = iota((256, LN), 0) & (LN - 1), iota((256, LN), 1)
    even = (dst & 1) == 0
    w_edge[...] = jnp.where((even & (src == LN - 1)) | ((dst & 1 == 1) & (src == 0)), 1.0, 0.0).astype(BF16)

    def keep(p, x):
        xs[pl.ds(pl.multiple_of(p * OY, OY), OY), :] = jnp.concatenate(split(x), axis=1)

    def group_rows(i):
        return pl.ds(pl.multiple_of(i * (2 * GROUP * OY), 2 * GROUP * OY), 2 * GROUP * OY)

    def edge_columns(i, acc):
        found = jnp.dot(xs[group_rows(i), :], w_edge[...], preferred_element_type=F32)
        for k in range(2 * GROUP):
            acc = jnp.where((lane48 >> 1) == i * 2 * GROUP + k, found[k * OY:(k + 1) * OY], acc)
        return acc

    def first_edges(i, accu):
        for j in range(GROUP):
            l = i * GROUP + j
            for t in range(2):
                p = 2 * l + t
                x = va[l, t, TOP:TOP + OY, :]
                keep(p, x)
                rsend[0, 0, pl.ds(p, 1), :] = x[OY - 1:OY]
                rsend[0, 1, pl.ds(p, 1), :] = x[0:1]
            accu = jnp.where(lane48 == l, pltpu.roll(u[l] * sea, l + 1, 1), accu)
            rsend[0, 0, pl.ds(PL + l, 1), :] = n[l, OY - 1:OY, :] * sea[OY - 1:OY]
        return accu

    zero48 = jnp.zeros((OY, LN), F32)
    accu = lax.fori_loop(0, LO // GROUP, first_edges, zero48)
    acc = lax.fori_loop(0, LO // GROUP, edge_columns, zero48)
    acc = jnp.where((lane48 >> 1) == PL, pltpu.roll(sea, 2 * PL + 1, 1), acc)
    csend[0, 0] = acc
    csend[0, 1] = accu
    rsend[0, 1, PL:96, :] = jnp.zeros((96 - PL, LN), F32)
    tail = jnp.where(iota((8, LN), 0) == 2, sea[OY - 1:OY], 0.0)
    rsend[0, 0, 88:96, :] = jnp.where(iota((8, LN), 0) < 2, rsend[0, 0, 88:96, :], tail)
    rsend[0, 1, 88:96, :] = jnp.where(iota((8, LN), 0) == 2, sea[0:1], 0.0)

    @pl.when(gy == 0)
    def _():
        for s in range(ADV):
            rrecv[s, 1] = jnp.zeros((96, LN), F32)

    pl.semaphore_wait(barrier, DEV - 1)

    east, west = lax.rem(gx + 1, GX), lax.rem(gx + GX - 1, GX)

    def lines(s):
        return 96 if s == 0 else 64

    def sides(s):
        return 2 if s == 0 else 1

    def row_copy(s, out, into, to):
        return pltpu.make_async_remote_copy(
            src_ref=rsend.at[s, out, 0:lines(s), :], dst_ref=rrecv.at[s, into, 0:lines(s), :],
            send_sem=hs_sem.at[s, out], recv_sem=hr_sem.at[s, into], device_id=to, device_id_type=MESH)

    def col_copy(s, out, into, to):
        return pltpu.make_async_remote_copy(
            src_ref=csend.at[s, 0:sides(s)], dst_ref=crecv.at[s, into, 0:sides(s)],
            send_sem=hs_sem.at[s, 2 + out], recv_sem=hr_sem.at[s, 2 + into], device_id=to, device_id_type=MESH)

    def send_edges(s):
        col_copy(s, 0, 0, (east, gy)).start()
        col_copy(s, 1, 1, (west, gy)).start()

        @pl.when(gy < GY - 1)
        def _():
            row_copy(s, 0, 1, (gx, gy + 1)).start()

        @pl.when(gy == GY - 1)
        def _():
            row_copy(s, 0, 0, (GX - 1 - gx, gy)).start()

        @pl.when(gy > 0)
        def _():
            row_copy(s, 1, 0, (gx, gy - 1)).start()

    flip = jnp.where(iota((LN, LN), 0) + iota((LN, LN), 1) == LN - 1, 1.0, 0.0)

    def await_edges(s):
        col_copy(s, 0, 0, (east, gy)).wait()
        col_copy(s, 1, 1, (west, gy)).wait()
        row_copy(s, 0, 0, (east, gy)).wait()

        @pl.when(gy > 0)
        def _():
            row_copy(s, 1, 1, (east, gy)).wait()

        @pl.when(gy == GY - 1)
        def _():
            rows = rrecv[s, 0, 0:lines(s), :]
            rrecv[s, 0, 0:lines(s), :] = jnp.dot(
                rows, flip, precision=lax.Precision.HIGHEST, preferred_element_type=F32)

    send_edges(0)

    def exchange_copy(k, snd_buf, rcv_buf, px, py):
        return pltpu.make_async_remote_copy(
            src_ref=snd_buf.at[px * GY + py], dst_ref=rcv_buf.at[me], send_sem=as_sem.at[k], recv_sem=ar_sem.at[k, gx],
            device_id=(px, py), device_id_type=MESH)

    def send_chunk(k, snd_buf, rcv_buf, c, start):
        def out(j, carry):
            exchange_copy(k, snd_buf, rcv_buf, c, lax.rem(gy + j, GY)).start()
            return carry

        lax.fori_loop(start, GY, out, 0)

    def exchange_wait(k, snd_buf, rcv_buf, c, blocks):
        return pltpu.make_async_remote_copy(
            src_ref=snd_buf.at[pl.ds(0, blocks)], dst_ref=rcv_buf.at[pl.ds(0, blocks)],
            send_sem=as_sem.at[k], recv_sem=ar_sem.at[k, c], device_id=(east, gy), device_id_type=MESH)

    def chunk_order(i):
        return lax.rem(gx + 1 + i, GX)

    def arrival_order(i):
        return lax.rem(gx + GX - 1 - i, GX)

    def await_chunk(k, snd_buf, rcv_buf, i):
        c = arrival_order(i)

        @pl.when(i < GX - 1)
        def _():
            exchange_wait(k, snd_buf, rcv_buf, c, GY).wait_recv()

        @pl.when(i == GX - 1)
        def _():
            exchange_wait(k, snd_buf, rcv_buf, c, GY - 1).wait_recv()

        return c

    def exchange_out(i, carry):
        send_chunk(0, send1, recv1, chunk_order(i), 0)
        return carry

    def exchange_part(s):
        begin, end = sum(SENDS[:s]), sum(SENDS[:s + 1])
        lax.fori_loop(begin, min(end, GX - 1), exchange_out, 0)
        if end == GX and SENDS[s] > 0:
            send_chunk(0, send1, recv1, gx, 1)

    exchange_part(0)
    recv1[me] = send1[me]

    for i in (6, 7, 8):
        loads[i].wait()
    rows3[0] = slot_rows(ti_v[...])
    snd = sb_v[...]
    rows3[2] = slot_rows(jnp.where(snd < 192, (snd & 3) * OY + (snd >> 2), -1))
    for c in range(8):
        whi, wlo = split(w_v[:, c * LN:(c + 1) * LN])
        both = jnp.concatenate([whi.astype(F32), wlo.astype(F32)], axis=0)
        w2t[0, c * LN:(c + 1) * LN, :] = both.T
    for b in range(B):
        w2t[1, b * B:(b + 1) * B, :] = w2t[0, pl.ds(b, B, stride=B), :]
    w2p[0] = w2t[0].astype(BF16)
    w2p[1] = w2t[1].astype(BF16)

    def hots(g, carry):
        rt = rows3[0, pl.ds(g, 1), :]
        oh_t[g] = jnp.where((sub128 & 63).astype(F32) == rt, 1.0, 0.0).astype(BF16)
        rs = rows3[2, pl.ds(g, 1), :]
        hot = jnp.where(iota((256, LN), 0).astype(F32) == rs, 1.0, 0.0)
        oh_h[g] = hot.astype(BF16)
        oh_ht[g, :, 0:LN] = hot[:LN].T.astype(BF16)
        oh_ht[g, :, LN:] = hot[LN:].T.astype(BF16)
        return carry

    lax.fori_loop(0, 16, hots, 0)

    def tiles(c, carry):
        hot = jnp.concatenate([oh_t[2 * c], oh_t[2 * c + 1]], axis=1)
        g1[c] = jnp.dot(w2p[0], hot, preferred_element_type=F32)
        g2[c] = jnp.dot(w2p[1], hot, preferred_element_type=F32)
        return carry

    lax.fori_loop(0, 2, tiles, 0)

    await_edges(0)


    def ghosts(s):
        even = (lane48 & 1) == 0
        return jnp.where(even, pltpu.roll(crecv[s, 1, 0], LN - 1, 1), pltpu.roll(crecv[s, 0, 0], 1, 1))

    gh = ghosts(0)
    last = lane48 == LN - 1
    first = lane48 == 0
    gsea = pltpu.roll(gh, LN - 1 - 2 * PL, 1)
    sea_e = jnp.where(last, gsea, pltpu.roll(sea, LN - 1, 1))
    sea_p[TOP + OY:TOP + OY + 1, :] = rrecv[0, 0, 90:91, :]
    sea_n = sea_p[TOP + 1:TOP + 1 + OY, :]
    open_e = sea * sea_e
    open_n = sea * sea_n
    uw_ghost = crecv[0, 0, 1] * jnp.broadcast_to(sea[:, 0:1], (OY, LN))

    def faces(i, carry):
        for j in range(GROUP):
            face(i * GROUP + j)
        return carry

    def face(l):
        um = u[l] * open_e
        uw = jnp.where(first, pltpu.roll(uw_ghost, lax.rem(LN - l, LN), 1), pltpu.roll(um, 1, 1))
        nm = n[l] * open_n
        below = rrecv[0, 1, pl.ds(PL + l, 1), :] * sea[0:1]
        ns = jnp.where(row48 == 0, below, pltpu.roll(nm, 1, 0))
        ce[l] = -jnp.minimum(um, 0.0)
        cw[l] = jnp.maximum(uw, 0.0)
        cn[l] = -jnp.minimum(nm, 0.0)
        cs[l] = jnp.maximum(ns, 0.0)
        c0[l] = 1.0 - jnp.maximum(um, 0.0) + jnp.minimum(uw, 0.0) - jnp.maximum(nm, 0.0) + jnp.minimum(ns, 0.0)

    lax.fori_loop(0, LO // GROUP, faces, 0)

    for s in range(ADV):
        if s > 0:
            lax.fori_loop(2 * s, 2 * s + 2, tiles, 0)
            await_edges(s)
        gh = ghosts(s)
        now, later = (va, vb) if s % 2 == 0 else (vb, va)

        def edges_in(i, carry, s=s, now=now):
            for j in range(GROUP):
                l = i * GROUP + j
                for t in range(2):
                    now[l, t, TOP - 1:TOP, :] = rrecv[s, 1, pl.ds(2 * l + t, 1), :]
                    now[l, t, TOP + OY:TOP + OY + 1, :] = rrecv[s, 0, pl.ds(2 * l + t, 1), :]
            return carry

        lax.fori_loop(0, LO // GROUP, edges_in, 0)
        ghi, glo = (x.astype(F32) for x in split(gh))

        def substep(i, carry, s=s, now=now, later=later, ghi=ghi, glo=glo):
            parts = []
            for k in range(2 * GROUP):
                own = (lane48 >> 1) == i * 2 * GROUP + k
                parts.append(jnp.concatenate(
                    [jnp.where(own, ghi, 0.0).astype(BF16), jnp.where(own, glo, 0.0).astype(BF16)], axis=1))
            near = jnp.dot(xs[group_rows(i), :], w_shift[...], preferred_element_type=F32)
            near = near + jnp.dot(jnp.concatenate(parts, axis=0), w_ghost[...], preferred_element_type=F32)
            for j in range(GROUP):
                l = i * GROUP + j
                k0, ke, kw, kn, ks = c0[l], ce[l], cw[l], cn[l], cs[l]
                for t in range(2):
                    k = 2 * j + t
                    rows = near[k * OY:(k + 1) * OY]
                    y = k0 * now[l, t, TOP:TOP + OY, :] + ke * rows[:, :LN] + kw * rows[:, LN:]
                    y = y + kn * now[l, t, TOP + 1:TOP + 1 + OY, :] + ks * now[l, t, TOP - 1:TOP - 1 + OY, :]
                    later[l, t, TOP:TOP + OY, :] = y
                    if s < ADV - 1:
                        p = 2 * l + t
                        keep(p, y)
                        rsend[s + 1, 0, pl.ds(p, 1), :] = y[OY - 1:OY]
                        rsend[s + 1, 1, pl.ds(p, 1), :] = y[0:1]
            return carry

        lax.fori_loop(0, LO // GROUP, substep, 0)
        if s < ADV - 1:
            csend[s + 1, 0] = lax.fori_loop(0, LO // GROUP, edge_columns, zero48)
            for k in range(2):
                rsend[s + 1, k, PL:64, :] = jnp.zeros((64 - PL, LN), F32)
            send_edges(s + 1)
            exchange_part(s + 1)

    loads[9].wait()

    def up(i, carry):
        e, yt, ys = carry
        l = LO - 2 - i
        k = kv[l] * sea
        inv = 1.0 / (e + k)
        r = k * inv
        elim_r[l + 1] = r
        elim_z[0, l + 1] = yt * inv
        elim_z[1, l + 1] = ys * inv
        return (1.0 + k * (1.0 - r), va[l, 0, TOP:TOP + OY, :] + r * yt, va[l, 1, TOP:TOP + OY, :] + r * ys)

    start = (jnp.ones((OY, LN), F32), va[LO - 1, 0, TOP:TOP + OY, :], va[LO - 1, 1, TOP:TOP + OY, :])
    e, yt, ys = lax.fori_loop(0, LO - 1, up, start)
    inv = 1.0 / e
    top_y[0], top_y[1], top_y[2] = yt, ys, inv

    loads[10].wait()
    loads[11].wait()

    def air_up(i, carry):
        e, y = carry
        l = LA - 2 - i
        k = ak_v[l + 1]
        inv = 1.0 / (e + k)
        r = k * inv
        air_r[l + 1] = r
        air_z[l + 1] = y * inv
        return 1.0 + k * (1.0 - r), at_v[l] + r * y

    ea, ya = lax.fori_loop(0, LA - 1, air_up, (jnp.ones((AY, LN), F32), at_v[LA - 1]))
    inv_a = 1.0 / (ea + ak_v[0])
    air_z[0] = ya
    air_r[0] = inv_a

    def apply_tiles(tile_ref, c, h):
        out = jnp.zeros((NF, B, LN), F32)
        for a in range(B):
            w = tile_ref[c, a * B:(a + 1) * B, h * LN:(h + 1) * LN]
            out = out + w[None] * xt[:, a:a + 1, :]
        return out.reshape(NF * B, LN)

    total[...] = jnp.zeros_like(total)

    def spread(i, carry):
        c = await_chunk(0, send1, recv1, i)
        parts = []
        for h in range(2):
            xt[...] = recv1[pl.ds(c * 16 + h * 8, 8)].reshape(LN, LN).T.reshape(NF, B, LN)
            parts.append(jnp.concatenate(split(apply_tiles(g1, c, h)), axis=0))
        total[...] += jnp.dot(
            jnp.concatenate(parts, axis=1), oh_ht[pl.ds(2 * c, 2)].reshape(CW, 256), preferred_element_type=F32)
        return carry

    lax.fori_loop(0, CHUNKS, spread, 0)

    both = total[0:LN, :] + total[LN:, :]
    landed = jnp.concatenate([both[:, :LN].T, both[:, LN:].T], axis=0)
    groups = [landed[q * OY:(q + 1) * OY] for q in range(4)]
    force = [blocks_to_field(groups, f) for f in range(NF)]

    xt0 = (top_y[0] + sea * force[0]) * top_y[2]
    xs0 = (top_y[1] + sea * force[1]) * top_y[2]
    surf = [
        sea * xt0,
        sea,
        sea * (u[0] + 0.1 * jnp.tanh(force[2])),
        sea * (n[0] + 0.1 * jnp.tanh(force[3])),
    ]
    sblocks = jnp.concatenate([fields_to_blocks(surf, q) for q in range(4)] + [jnp.zeros((64, LN), F32)], axis=0)
    lifted = jnp.concatenate([sblocks[:LN].T, sblocks[LN:].T], axis=1)
    lhi, llo = split(lifted)
    st[...] = jnp.concatenate([lhi, llo], axis=0)

    def push(i, carry):
        c = chunk_order(i)
        for h in range(2):
            g = 2 * c + h
            two = jnp.dot(st[...], oh_h[g], preferred_element_type=F32)
            xt[...] = (two[:LN] + two[LN:]).reshape(NF, B, LN)
            send2[pl.ds(g * 8, 8)] = apply_tiles(g2, c, h).T.reshape(8, CAP, LN)

        @pl.when(i < GX - 1)
        def _():
            send_chunk(1, send2, recv2, c, 0)

        @pl.when(i == GX - 1)
        def _():
            send_chunk(1, send2, recv2, c, 1)

        return carry

    lax.fori_loop(0, GX, push, 0)
    recv2[me] = send2[me]

    x_out[0] = xt0
    x_out[LO] = xs0

    def down(l, carry):
        a, b = carry
        r = elim_r[l]
        a = elim_z[0, l] + r * a
        b = elim_z[1, l] + r * b
        x_out[l] = a
        x_out[LO + l] = b
        return a, b

    lax.fori_loop(1, LO, down, (xt0, xs0))
    store = pltpu.make_async_copy(x_out, out_tr, out_sem)
    store.start()

    def gather(i, carry):
        c = await_chunk(1, send2, recv2, i)
        for h in range(2):
            g = 2 * c + h
            hi, lo = split(recv2[pl.ds(g * 8, 8)].reshape(LN, LN))
            carry = carry + jnp.dot(oh_b[g], jnp.concatenate([hi, lo], axis=1), preferred_element_type=F32)
        return carry

    both = lax.fori_loop(0, GX, gather, jnp.zeros((64, 256), F32))
    landed = both[:, :LN] + both[:, LN:]
    groups = [landed[q * AY:(q + 1) * AY] for q in range(4)]
    fields = [blocks_to_field(groups, f) for f in range(NF)]
    for f in range(NF):
        out_sf[f] = fields[f]
    ground = at_v[0] * (1.0 - fields[1]) + fields[0]
    x = (air_z[0] + ak_v[0] * ground) * air_r[0]
    out_air[0] = x
    for l in range(1, LA):
        x = air_z[l] + air_r[l] * x
        out_air[l] = x

    exchange_wait(0, send1, recv1, gx, DEV - 1).wait_send()
    exchange_wait(1, send2, recv2, gx, DEV - 1).wait_send()
    store.wait()


def hand_on(tr, air, sf, out_tr, out_air, out_sf, tr_v, air_v, sf_v, sem_in, sem_out):
    step = PL // PARTS
    parts = [pl.ds(i * step, step) for i in range(PARTS)]
    trios = [(tr.at[p], tr_v.at[p], out_tr.at[p]) for p in parts] + [(air, air_v, out_air), (sf, sf_v, out_sf)]
    ins = [pltpu.make_async_copy(a, b, sem_in.at[i]) for i, (a, b, _) in enumerate(trios)]
    outs = [pltpu.make_async_copy(b, c, sem_out.at[i]) for i, (_, b, c) in enumerate(trios)]
    for copy in ins:
        copy.start()
    for copy, back in zip(ins, outs):
        copy.wait()
        back.start()
    for back in outs:
        back.wait()


def shards(
    tracers, east_flow, north_flow, ocean_kappa, land_sea, air_temp, air_kappa, air_fluxes,
    weight_tiles, tile_index, send_blocks, receive_blocks,
):
    anyspace = pl.BlockSpec(memory_space=pl.ANY)
    vm = pl.BlockSpec(memory_space=pltpu.VMEM)
    V = pltpu.VMEM
    scratch = [
        V((LO, 2, 64, LN), F32), V((LO, 2, 64, LN), F32), V((PL * OY, 256), BF16), V((256, 256), BF16), V((256, 256), BF16),
        V((256, LN), BF16), V((LO, OY, LN), F32), V((LO, OY, LN), F32), V((LO - 1, OY, LN), F32),
        V((OY, LN), jnp.int32), V((64, LN), F32), V((LA, AY, LN), F32), V((LA, AY, LN), F32), V((NF, AY, LN), F32),
        V((64, 1024), F32), V((CAP, DEV), jnp.int32), V((CAP, DEV), jnp.int32), V((CAP, DEV), jnp.int32),
        V((3, 16, LN), F32), V((2, 1024, LN), F32), V((2, 1024, LN), BF16),
        V((16, LN, LN), BF16), V((16, 256, LN), BF16), V((16, LN, 256), BF16),
        V((16, 64, LN), BF16),
        V((CHUNKS, 1024, CW), F32), V((CHUNKS, 1024, CW), F32),
        V((DEV, CAP, LN), F32), V((DEV, CAP, LN), F32), V((DEV, CAP, LN), F32), V((DEV, CAP, LN), F32),
        V((NF, B, LN), F32), V((256, 256), F32), V((256, 256), BF16),
        V((ADV, 2, 96, LN), F32), V((ADV, 2, 96, LN), F32), V((ADV, 2, OY, LN), F32), V((ADV, 2, 2, OY, LN), F32),
        V((LO, OY, LN), F32), V((LO, OY, LN), F32), V((LO, OY, LN), F32), V((LO, OY, LN), F32), V((LO, OY, LN), F32),
        V((LO, OY, LN), F32), V((2, LO, OY, LN), F32), V((3, OY, LN), F32), V((LA, AY, LN), F32), V((LA, AY, LN), F32),
        V((PL, OY, LN), F32),
        pltpu.SemaphoreType.DMA((13,)), pltpu.SemaphoreType.DMA, pltpu.SemaphoreType.DMA((ADV, 4)),
        pltpu.SemaphoreType.DMA((ADV, 4)), pltpu.SemaphoreType.DMA((2,)), pltpu.SemaphoreType.DMA((2, GX)),
    ]
    out_tr, out_air, out_sf = pl.pallas_call(
        kernel,
        out_shape=(
            jax.ShapeDtypeStruct((PL, OY, LN), F32),
            jax.ShapeDtypeStruct((LA, AY, LN), F32),
            jax.ShapeDtypeStruct((NF, AY, LN), F32),
        ),
        in_specs=[anyspace] * 12,
        out_specs=(anyspace, vm, vm),
        scratch_shapes=scratch,
        compiler_params=pltpu.CompilerParams(
            collective_id=0, has_side_effects=True, vmem_limit_bytes=60 * 1024 * 1024),
        name="coupling_step",
    )(
        tracers, east_flow, north_flow, ocean_kappa, land_sea, air_temp, air_kappa, air_fluxes,
        weight_tiles, *(jnp.swapaxes(x, 1, 2) for x in (tile_index, send_blocks, receive_blocks)),
    )
    out_tr, out_air, out_sf = pl.pallas_call(
        hand_on,
        out_shape=(
            jax.ShapeDtypeStruct((PL, OY, LN), F32),
            jax.ShapeDtypeStruct((LA, AY, LN), F32),
            jax.ShapeDtypeStruct((NF, AY, LN), F32),
        ),
        in_specs=[anyspace] * 3,
        out_specs=[anyspace] * 3,
        scratch_shapes=[
            V((PL, OY, LN), F32), V((LA, AY, LN), F32), V((NF, AY, LN), F32),
            pltpu.SemaphoreType.DMA((PARTS + 2,)), pltpu.SemaphoreType.DMA((PARTS + 2,)),
        ],
        compiler_params=pltpu.CompilerParams(vmem_limit_bytes=60 * 1024 * 1024),
        name="hand_on",
    )(out_tr, out_air, out_sf)
    return out_tr.reshape(2, LO, OY, LN), out_air, out_sf


def solution(mesh):
    return jax.shard_map(
        shards,
        mesh=mesh,
        in_specs=(
            P(None, None, "gy", "gx"),
            P(None, "gy", "gx"),
            P(None, "gy", "gx"),
            P(None, "gy", "gx"),
            P("gy", "gx"),
            P(None, "gy", "gx"),
            P(None, "gy", "gx"),
            P(None, "gy", "gx"),
            P(("gx", "gy"), None, None),
            P(("gx", "gy"), None, None),
            P(("gx", "gy"), None, None),
            P(("gx", "gy"), None, None),
        ),
        out_specs=(P(None, None, "gy", "gx"), P(None, "gy", "gx"), P(None, "gy", "gx")),
        check_vma=False,
    )
```

```python
import jax
import jax.numpy as jnp
from jax import lax
from jax.experimental import pallas as pl
from jax.experimental.pallas import tpu as pltpu
from jax.sharding import PartitionSpec as P

F32 = jnp.float32
BF16 = jnp.bfloat16
MESH = pl.DeviceIdType.MESH
NF, B, CAP, ADV = 4, 32, 16, 4
GX, GY = 8, 16
DEV = GX * GY
SLOTS = DEV * CAP
LO, LA, OY, AY, LN = 30, 16, 48, 16, 128
PL = 2 * LO
TOP = 8
CHUNKS, CW = 8, 256
GROUP = 10
SENDS = (3, 3, 2)
PARTS = 6
UNROLL = 2


def iota(shape, dim):
    return lax.broadcasted_iota(jnp.int32, shape, dim)


def split(x):
    hi = x.astype(BF16)
    return hi, (x - hi.astype(F32)).astype(BF16)


def fields_to_blocks(fields, q):
    lane = iota(fields[0].shape, 1) >> 5
    out = jnp.zeros_like(fields[0])
    for f in range(len(fields)):
        moved = pltpu.roll(fields[f], ((f - q) * B) % LN, 1) if f != q else fields[f]
        out = jnp.where(lane == f, moved, out)
    return out


def blocks_to_field(groups, f):
    lane = iota(groups[0].shape, 1) >> 5
    out = jnp.zeros_like(groups[0])
    for q in range(4):
        moved = pltpu.roll(groups[q], ((q - f) * B) % LN, 1) if f != q else groups[q]
        out = jnp.where(lane == q, moved, out)
    return out


def slot_rows(idx):
    lane = iota((CAP, LN), 1)
    spread = 2 * (lane & 7) + (lane >> 6) == iota((CAP, LN), 0)
    tiled = jnp.dot(idx.astype(F32).T.astype(BF16), spread.astype(F32).astype(BF16), preferred_element_type=F32)
    own = ((iota((DEV, LN), 1) >> 3) & 7) == (iota((DEV, LN), 0) & 7)
    return jnp.sum(jnp.where(own, tiled, 0.0).reshape(16, 8, LN), axis=1)


def mix_halves(a, b):
    low = iota(a.shape, 1) < 64
    return jnp.where(low, a, pltpu.roll(b, 64, 1)), jnp.where(low, pltpu.roll(a, 64, 1), b)


def pack(a, b):
    return jnp.concatenate(mix_halves(a, b), axis=0).T


def unpack(rows):
    turned = rows.T
    return mix_halves(turned[:64], turned[64:])


def kernel(
    tr, ue, un, kap, land, atemp, akap, aflux, wts, tix, sbl, rbl,
    out_tr, out_air, out_sf,
    va, vb, xs, w_shift, w_edge, u, n, kv, land_v, sea_p, at_v, ak_v, af_v, w_v, ti_v, sb_v, rb_v,
    rows3, w2t, w2p, oh_t, oh_h, oh_ht, oh_b, g1, g2,
    box_out, box_in, xt, total, st,
    rsend, rrecv, csend, crecv,
    c0, ce, cw, cn, cs, elim_r, elim_z, top_y, air_r, air_z, x_out,
    in_sem, out_sem, hs_sem, hr_sem, as_sem, ar_sem,
):
    gx = lax.axis_index("gx")
    gy = lax.axis_index("gy")
    me = gx * GY + gy

    pairs = (
        (aflux, af_v), (rbl.at[0], rb_v), (land, land_v), (tr.at[0], va.at[:, 0, TOP:TOP + OY, :]), (ue, u), (un, n),
        (wts.at[0], w_v), (tix.at[0], ti_v), (sbl.at[0], sb_v), (kap, kv), (atemp, at_v), (akap, ak_v),
        (tr.at[1], va.at[:, 1, TOP:TOP + OY, :]),
    )
    loads = [pltpu.make_async_copy(s, d, in_sem.at[i]) for i, (s, d) in enumerate(pairs)]
    for c in loads:
        c.start()

    barrier = pltpu.get_barrier_semaphore()

    def greet(i, carry):
        pl.semaphore_signal(
            barrier, inc=1, device_id=(lax.rem(gx + lax.div(i, GY), GX), lax.rem(gy + lax.rem(i, GY), GY)),
            device_id_type=MESH)
        return carry

    lax.fori_loop(1, DEV, greet, 0)

    lane48 = iota((OY, LN), 1)
    row48 = iota((OY, LN), 0)

    loads[0].wait()
    loads[1].wait()
    tgt = rb_v[...]
    tgt = jnp.where(tgt < 64, (tgt & 3) * AY + (tgt >> 2), -1)
    rows3[1] = slot_rows(tgt)
    air = [af_v[f] for f in range(NF)]
    blocks = jnp.concatenate([fields_to_blocks(air, q) for q in range(4)], axis=0)
    bhi, blo = split(blocks)
    blocks2 = jnp.concatenate([bhi.astype(F32), blo.astype(F32)], axis=0).T.astype(BF16)
    sub128 = iota((LN, LN), 0)

    def pick(c, carry):
        hot = [jnp.where((sub128 & 63).astype(F32) == rows3[1, pl.ds(2 * c + h, 1), :], 1.0, 0.0) for h in range(2)]
        oh_b[c] = jnp.concatenate(mix_halves(hot[0][:64], hot[1][:64]), axis=0).astype(BF16)
        picked = jnp.dot(blocks2, jnp.concatenate(hot, axis=1).astype(BF16), preferred_element_type=F32)
        a, b = picked[:, :LN], picked[:, LN:]
        box_out[0, pl.ds(c * 16, 16)] = pack(a[64:], b[64:]).reshape(16, 8, LN)
        box_out[1, pl.ds(c * 16, 16)] = pack(a[:64], b[:64]).reshape(16, 8, LN)
        return carry

    lax.fori_loop(0, CHUNKS, pick, 0)
    box_in[0, me] = box_out[0, me]
    box_in[1, me] = box_out[1, me]

    for i in (2, 3, 4, 5, 12):
        loads[i].wait()
    sea = land_v[...].astype(F32)
    sea_p[TOP:TOP + OY, :] = sea

    src, dst = iota((256, 256), 0) & (LN - 1), iota((256, 256), 1)
    to_east = (src == dst + 1) & (dst < LN - 1)
    to_west = (src == dst - 1 - LN) & (dst > LN)
    w_shift[0:256, :] = jnp.where(to_east | to_west, 1.0, 0.0).astype(BF16)
    even = (src & 1) == 0
    w_shift[256:512, :] = jnp.where((even & (dst == LN - 1)) | ((src & 1 == 1) & (dst == LN)), 1.0, 0.0).astype(BF16)
    src, dst = iota((256, LN), 0) & (LN - 1), iota((256, LN), 1)
    even = (dst & 1) == 0
    w_edge[...] = jnp.where((even & (src == LN - 1)) | ((dst & 1 == 1) & (src == 0)), 1.0, 0.0).astype(BF16)

    def keep(p, x):
        xs[pl.ds(pl.multiple_of(p * OY, OY), OY), :] = jnp.concatenate(split(x), axis=1)

    def group_rows(i):
        return pl.ds(pl.multiple_of(i * (2 * GROUP * OY), 2 * GROUP * OY), 2 * GROUP * OY)

    def edge_columns():
        acc = jnp.zeros((OY, LN), F32)
        for i in range(LO // GROUP):
            found = jnp.dot(xs[group_rows(i), :], w_edge[...], preferred_element_type=F32)
            for k in range(2 * GROUP):
                acc = jnp.where((lane48 >> 1) == i * 2 * GROUP + k, found[k * OY:(k + 1) * OY], acc)
        return acc

    def first_edges(i, accu):
        for j in range(GROUP):
            l = i * GROUP + j
            for t in range(2):
                p = 2 * l + t
                x = va[l, t, TOP:TOP + OY, :]
                keep(p, x)
                rsend[0, 0, pl.ds(p, 1), :] = x[OY - 1:OY]
                rsend[0, 1, pl.ds(p, 1), :] = x[0:1]
            accu = jnp.where(lane48 == l, pltpu.roll(u[l] * sea, l + 1, 1), accu)
            rsend[0, 0, pl.ds(PL + l, 1), :] = n[l, OY - 1:OY, :] * sea[OY - 1:OY]
        return accu

    zero48 = jnp.zeros((OY, LN), F32)
    accu = lax.fori_loop(0, LO // GROUP, first_edges, zero48)
    acc = edge_columns()
    acc = jnp.where((lane48 >> 1) == PL, pltpu.roll(sea, 2 * PL + 1, 1), acc)
    csend[0, 0] = acc
    csend[0, 1] = accu
    rsend[0, 1, PL:96, :] = jnp.zeros((96 - PL, LN), F32)
    tail = jnp.where(iota((8, LN), 0) == 2, sea[OY - 1:OY], 0.0)
    rsend[0, 0, 88:96, :] = jnp.where(iota((8, LN), 0) < 2, rsend[0, 0, 88:96, :], tail)
    rsend[0, 1, 88:96, :] = jnp.where(iota((8, LN), 0) == 2, sea[0:1], 0.0)

    @pl.when(gy == 0)
    def _():
        for s in range(ADV):
            rrecv[s, 1] = jnp.zeros((96, LN), F32)

    pl.semaphore_wait(barrier, DEV - 1)

    east, west = lax.rem(gx + 1, GX), lax.rem(gx + GX - 1, GX)

    def lines(s):
        return 96 if s == 0 else 64

    def sides(s):
        return 2 if s == 0 else 1

    def row_copy(s, out, into, to):
        return pltpu.make_async_remote_copy(
            src_ref=rsend.at[s, out, 0:lines(s), :], dst_ref=rrecv.at[s, into, 0:lines(s), :],
            send_sem=hs_sem.at[s, out], recv_sem=hr_sem.at[s, into], device_id=to, device_id_type=MESH)

    def col_copy(s, out, into, to):
        return pltpu.make_async_remote_copy(
            src_ref=csend.at[s, 0:sides(s)], dst_ref=crecv.at[s, into, 0:sides(s)],
            send_sem=hs_sem.at[s, 2 + out], recv_sem=hr_sem.at[s, 2 + into], device_id=to, device_id_type=MESH)

    def send_edges(s):
        col_copy(s, 0, 0, (east, gy)).start()
        col_copy(s, 1, 1, (west, gy)).start()

        @pl.when(gy < GY - 1)
        def _():
            row_copy(s, 0, 1, (gx, gy + 1)).start()

        @pl.when(gy == GY - 1)
        def _():
            row_copy(s, 0, 0, (GX - 1 - gx, gy)).start()

        @pl.when(gy > 0)
        def _():
            row_copy(s, 1, 0, (gx, gy - 1)).start()

    flip = jnp.where(iota((LN, LN), 0) + iota((LN, LN), 1) == LN - 1, 1.0, 0.0)

    def await_edges(s):
        col_copy(s, 0, 0, (east, gy)).wait()
        col_copy(s, 1, 1, (west, gy)).wait()
        row_copy(s, 0, 0, (east, gy)).wait()

        @pl.when(gy > 0)
        def _():
            row_copy(s, 1, 1, (east, gy)).wait()

        @pl.when(gy == GY - 1)
        def _():
            rows = rrecv[s, 0, 0:lines(s), :]
            rrecv[s, 0, 0:lines(s), :] = jnp.dot(
                rows, flip, precision=lax.Precision.HIGHEST, preferred_element_type=F32)

    send_edges(0)

    def send_chunk(k, c, start):
        def out(j, carry):
            py = lax.rem(gy + j, GY)
            pltpu.make_async_remote_copy(
                src_ref=box_out.at[k, c * GY + py], dst_ref=box_in.at[k, me], send_sem=as_sem.at[k],
                recv_sem=ar_sem.at[k, gx], device_id=(c, py), device_id_type=MESH).start()
            return carry

        lax.fori_loop(start, GY, out, 0)

    def exchange_wait(k, c, blocks):
        return pltpu.make_async_remote_copy(
            src_ref=box_out.at[k, pl.ds(0, blocks)], dst_ref=box_in.at[k, pl.ds(0, blocks)],
            send_sem=as_sem.at[k], recv_sem=ar_sem.at[k, c], device_id=(east, gy), device_id_type=MESH)

    def chunk_order(i):
        return lax.rem(gx + 1 + i, GX)

    def await_chunk(k, i):
        c = lax.rem(gx + GX - 1 - i, GX)

        @pl.when(i < GX - 1)
        def _():
            exchange_wait(k, c, GY).wait_recv()

        @pl.when(i == GX - 1)
        def _():
            exchange_wait(k, c, GY - 1).wait_recv()

        return c

    def exchange_part(k, begin, end):
        def out(i, carry):
            send_chunk(k, chunk_order(i), 0)
            return carry

        if begin < min(end, GX - 1):
            lax.fori_loop(begin, min(end, GX - 1), out, 0)
        if begin < end == GX:
            send_chunk(k, gx, 1)

    exchange_part(0, 0, GX)

    for i in (6, 7, 8):
        loads[i].wait()
    rows3[0] = slot_rows(ti_v[...])
    snd = sb_v[...]
    rows3[2] = slot_rows(jnp.where(snd < 192, (snd & 3) * OY + (snd >> 2), -1))
    for c in range(8):
        whi, wlo = split(w_v[:, c * LN:(c + 1) * LN])
        both = jnp.concatenate([whi.astype(F32), wlo.astype(F32)], axis=0)
        w2t[c * LN:(c + 1) * LN, :] = both.T
    w2p[0] = w2t[...].astype(BF16)
    for b in range(B):
        w2p[1, b * B:(b + 1) * B, :] = w2t[pl.ds(b, B, stride=B), :].astype(BF16)

    def hots(g, carry):
        rt = rows3[0, pl.ds(g, 1), :]
        oh_t[g] = jnp.where((sub128 & 63).astype(F32) == rt, 1.0, 0.0).astype(BF16)
        rs = rows3[2, pl.ds(g, 1), :]
        hot = jnp.where(iota((256, LN), 0).astype(F32) == rs, 1.0, 0.0)
        oh_h[g] = hot.astype(BF16)
        oh_ht[g, :, 0:LN] = hot[:LN].T.astype(BF16)
        oh_ht[g, :, LN:] = hot[LN:].T.astype(BF16)
        return carry

    lax.fori_loop(0, 16, hots, 0)

    def tiles(which, out):
        def one(c, carry):
            hot = jnp.concatenate([oh_t[2 * c], oh_t[2 * c + 1]], axis=1)
            out[c] = jnp.dot(w2p[which], hot, preferred_element_type=F32)
            return carry

        lax.fori_loop(0, CHUNKS, one, 0)

    tiles(0, g1)

    await_edges(0)


    def ghosts(s):
        even = (lane48 & 1) == 0
        return jnp.where(even, pltpu.roll(crecv[s, 1, 0], LN - 1, 1), pltpu.roll(crecv[s, 0, 0], 1, 1))

    gh = ghosts(0)
    last = lane48 == LN - 1
    first = lane48 == 0
    gsea = pltpu.roll(gh, LN - 1 - 2 * PL, 1)
    sea_e = jnp.where(last, gsea, pltpu.roll(sea, LN - 1, 1))
    sea_p[TOP + OY:TOP + OY + 1, :] = rrecv[0, 0, 90:91, :]
    sea_n = sea_p[TOP + 1:TOP + 1 + OY, :]
    open_e = sea * sea_e
    open_n = sea * sea_n
    uw_ghost = crecv[0, 0, 1] * jnp.broadcast_to(sea[:, 0:1], (OY, LN))

    def faces(i, carry):
        for j in range(GROUP):
            face(i * GROUP + j)
        return carry

    def face(l):
        um = u[l] * open_e
        uw = jnp.where(first, pltpu.roll(uw_ghost, lax.rem(LN - l, LN), 1), pltpu.roll(um, 1, 1))
        nm = n[l] * open_n
        below = rrecv[0, 1, pl.ds(PL + l, 1), :] * sea[0:1]
        ns = jnp.where(row48 == 0, below, pltpu.roll(nm, 1, 0))
        ce[l] = -jnp.minimum(um, 0.0)
        cw[l] = jnp.maximum(uw, 0.0)
        cn[l] = -jnp.minimum(nm, 0.0)
        cs[l] = jnp.maximum(ns, 0.0)
        c0[l] = 1.0 - jnp.maximum(um, 0.0) + jnp.minimum(uw, 0.0) - jnp.maximum(nm, 0.0) + jnp.minimum(ns, 0.0)

    lax.fori_loop(0, LO // GROUP, faces, 0)

    def apply_tiles(tile_ref, c, h, slot):
        out = jnp.zeros((2, B, LN), F32)
        for a in range(B):
            w = tile_ref[c, a * B:(a + 1) * B, h * LN:(h + 1) * LN]
            out = out + w[None] * xt[slot, :, a:a + 1, :]
        return out.reshape(2 * B, LN)

    def forcing(e):
        total[...] = jnp.zeros_like(total)

        def arrive(i, carry):
            await_chunk(e, i)
            return carry

        lax.fori_loop(0, CHUNKS, arrive, 0)

        def spread(i, carry):
            for d in range(UNROLL):
                c = i * UNROLL + d
                for h, x in enumerate(unpack(box_in[e, pl.ds(c * 16, 16)].reshape(LN, LN))):
                    xt[2 * d + h] = x.reshape(2, B, LN)
            parts = []
            for d in range(UNROLL):
                c = i * UNROLL + d
                for h in range(2):
                    parts.append(jnp.concatenate(split(apply_tiles(g1, c, h, 2 * d + h)), axis=0))
            total[...] += jnp.dot(
                jnp.concatenate(parts, axis=1), oh_ht[pl.ds(2 * UNROLL * i, 2 * UNROLL)].reshape(UNROLL * CW, 256),
                preferred_element_type=F32)
            return carry

        lax.fori_loop(0, CHUNKS // UNROLL, spread, 0)
        both = jnp.concatenate([total[0:64, :] + total[64:, :], jnp.zeros((64, 256), F32)], axis=0)
        landed = jnp.concatenate([both[:, :LN].T, both[:, LN:].T], axis=0)
        groups = [landed[q * OY:(q + 1) * OY] for q in range(4)]
        return [blocks_to_field(groups, f) for f in range(2)]

    def lift(surf):
        sblocks = jnp.concatenate([fields_to_blocks(surf, q) for q in range(4)] + [jnp.zeros((64, LN), F32)], axis=0)
        lifted = jnp.concatenate([sblocks[:LN].T[:64], sblocks[LN:].T[:64]], axis=1)
        st[...] = jnp.concatenate(split(lifted), axis=0)

    def send_terms(e):
        k = 2 + e

        def push(i, carry):
            chunks = [chunk_order(i * UNROLL + d) for d in range(UNROLL)]
            for d, c in enumerate(chunks):
                for h in range(2):
                    two = jnp.dot(st[...], oh_h[2 * c + h], preferred_element_type=F32)
                    xt[2 * d + h] = (two[:64] + two[64:]).reshape(2, B, LN)
            for d, c in enumerate(chunks):
                parts = [apply_tiles(g2, c, h, 2 * d + h) for h in range(2)]
                box_out[k, pl.ds(c * 16, 16)] = pack(*parts).reshape(16, 8, LN)
            for d, c in enumerate(chunks):
                if d < UNROLL - 1:
                    send_chunk(k, c, 0)
                    continue

                @pl.when(i < GX // UNROLL - 1)
                def _():
                    send_chunk(k, c, 0)

                @pl.when(i == GX // UNROLL - 1)
                def _():
                    send_chunk(k, c, 1)

            return carry

        lax.fori_loop(0, GX // UNROLL, push, 0)
        box_in[k, me] = box_out[k, me]

    def gather(e):
        def add(i, carry):
            c = await_chunk(2 + e, i)
            rows = box_in[2 + e, pl.ds(c * 16, 16)].reshape(LN, LN)
            return carry + jnp.dot(oh_b[c], jnp.concatenate(split(rows), axis=1), preferred_element_type=F32)

        both = lax.fori_loop(0, GX, add, jnp.zeros((LN, 256), F32))
        both = both[:, :LN] + both[:, LN:]
        landed = both[:64] + pltpu.roll(both[64:], 64, 1)
        groups = [landed[q * AY:(q + 1) * AY] for q in range(4)]
        return [blocks_to_field(groups, f) for f in range(2)]

    def before_wait(s):
        if s == 1:
            tiles(1, g2)
        if s == 2:
            f2, f3 = forcing(0)
            lift([sea * (u[0] + 0.1 * jnp.tanh(f2)), sea * (n[0] + 0.1 * jnp.tanh(f3))])
        if s == 3:
            send_terms(0)

    for s in range(ADV):
        if s > 0:
            before_wait(s)
            await_edges(s)
        gh = ghosts(s)
        now, later = (va, vb) if s % 2 == 0 else (vb, va)

        def edges_in(i, carry, s=s, now=now):
            for j in range(GROUP):
                l = i * GROUP + j
                for t in range(2):
                    now[l, t, TOP - 1:TOP, :] = rrecv[s, 1, pl.ds(2 * l + t, 1), :]
                    now[l, t, TOP + OY:TOP + OY + 1, :] = rrecv[s, 0, pl.ds(2 * l + t, 1), :]
            return carry

        lax.fori_loop(0, LO // GROUP, edges_in, 0)
        ghi, glo = (x.astype(F32) for x in split(gh))

        def substep(i, carry, s=s, now=now, later=later, ghi=ghi, glo=glo):
            parts = []
            for k in range(2 * GROUP):
                own = (lane48 >> 1) == i * 2 * GROUP + k
                parts.append(jnp.concatenate(
                    [jnp.where(own, ghi, 0.0).astype(BF16), jnp.where(own, glo, 0.0).astype(BF16)], axis=1))
            near = jnp.dot(
                jnp.concatenate([xs[group_rows(i), :], jnp.concatenate(parts, axis=0)], axis=1), w_shift[...],
                preferred_element_type=F32)
            for j in range(GROUP):
                l = i * GROUP + j
                k0, ke, kw, kn, ks = c0[l], ce[l], cw[l], cn[l], cs[l]
                for t in range(2):
                    k = 2 * j + t
                    rows = near[k * OY:(k + 1) * OY]
                    y = k0 * now[l, t, TOP:TOP + OY, :] + ke * rows[:, :LN] + kw * rows[:, LN:]
                    y = y + kn * now[l, t, TOP + 1:TOP + 1 + OY, :] + ks * now[l, t, TOP - 1:TOP - 1 + OY, :]
                    later[l, t, TOP:TOP + OY, :] = y
                    if s < ADV - 1:
                        p = 2 * l + t
                        keep(p, y)
                        rsend[s + 1, 0, pl.ds(p, 1), :] = y[OY - 1:OY]
                        rsend[s + 1, 1, pl.ds(p, 1), :] = y[0:1]
            return carry

        lax.fori_loop(0, LO // GROUP, substep, 0)
        if s < ADV - 1:
            csend[s + 1, 0] = edge_columns()
            for k in range(2):
                rsend[s + 1, k, PL:64, :] = jnp.zeros((64 - PL, LN), F32)
            send_edges(s + 1)
            exchange_part(1, sum(SENDS[:s]), sum(SENDS[:s + 1]))

    loads[9].wait()

    def up(i, carry):
        e, yt, ys = carry
        l = LO - 2 - i
        k = kv[l] * sea
        inv = 1.0 / (e + k)
        r = k * inv
        elim_r[l + 1] = r
        elim_z[0, l + 1] = yt * inv
        elim_z[1, l + 1] = ys * inv
        return (1.0 + k * (1.0 - r), va[l, 0, TOP:TOP + OY, :] + r * yt, va[l, 1, TOP:TOP + OY, :] + r * ys)

    start = (jnp.ones((OY, LN), F32), va[LO - 1, 0, TOP:TOP + OY, :], va[LO - 1, 1, TOP:TOP + OY, :])
    e, yt, ys = lax.fori_loop(0, LO - 1, up, start)
    inv = 1.0 / e
    top_y[0], top_y[1], top_y[2] = yt, ys, inv

    loads[10].wait()
    loads[11].wait()

    def air_up(i, carry):
        e, y = carry
        l = LA - 2 - i
        k = ak_v[l + 1]
        inv = 1.0 / (e + k)
        r = k * inv
        air_r[l + 1] = r
        air_z[l + 1] = y * inv
        return 1.0 + k * (1.0 - r), at_v[l] + r * y

    ea, ya = lax.fori_loop(0, LA - 1, air_up, (jnp.ones((AY, LN), F32), at_v[LA - 1]))
    inv_a = 1.0 / (ea + ak_v[0])
    air_z[0] = ya
    air_r[0] = inv_a

    f0, f1 = forcing(1)
    xt0 = (top_y[0] + sea * f0) * top_y[2]
    xs0 = (top_y[1] + sea * f1) * top_y[2]
    lift([sea * xt0, sea])
    send_terms(1)

    x_out[0] = xt0
    x_out[LO] = xs0

    def down(l, carry):
        a, b = carry
        r = elim_r[l]
        a = elim_z[0, l] + r * a
        b = elim_z[1, l] + r * b
        x_out[l] = a
        x_out[LO + l] = b
        return a, b

    lax.fori_loop(1, LO, down, (xt0, xs0))
    store = pltpu.make_async_copy(x_out, out_tr, out_sem)
    store.start()

    late = gather(0)
    fields = gather(1) + late
    for f in range(NF):
        out_sf[f] = fields[f]
    ground = at_v[0] * (1.0 - fields[1]) + fields[0]
    x = (air_z[0] + ak_v[0] * ground) * air_r[0]
    out_air[0] = x
    for l in range(1, LA):
        x = air_z[l] + air_r[l] * x
        out_air[l] = x

    for k in range(4):
        exchange_wait(k, gx, DEV - 1).wait_send()
    store.wait()


def hand_on(tr, air, sf, out_tr, out_air, out_sf, tr_v, air_v, sf_v, sem_in, sem_out):
    step = PL // PARTS
    parts = [pl.ds(i * step, step) for i in range(PARTS)]
    trios = [(tr.at[p], tr_v.at[p], out_tr.at[p]) for p in parts] + [(air, air_v, out_air), (sf, sf_v, out_sf)]
    ins = [pltpu.make_async_copy(a, b, sem_in.at[i]) for i, (a, b, _) in enumerate(trios)]
    outs = [pltpu.make_async_copy(b, c, sem_out.at[i]) for i, (_, b, c) in enumerate(trios)]
    for copy in ins:
        copy.start()
    for copy, back in zip(ins, outs):
        copy.wait()
        back.start()
    for back in outs:
        back.wait()


def shards(
    tracers, east_flow, north_flow, ocean_kappa, land_sea, air_temp, air_kappa, air_fluxes,
    weight_tiles, tile_index, send_blocks, receive_blocks,
):
    anyspace = pl.BlockSpec(memory_space=pl.ANY)
    vm = pl.BlockSpec(memory_space=pltpu.VMEM)
    V = pltpu.VMEM
    scratch = [
        V((LO, 2, 64, LN), F32), V((LO, 2, 64, LN), F32), V((PL * OY, 256), BF16), V((512, 256), BF16),
        V((256, LN), BF16), V((LO, OY, LN), F32), V((LO, OY, LN), F32), V((LO - 1, OY, LN), F32),
        V((OY, LN), jnp.int32), V((64, LN), F32), V((LA, AY, LN), F32), V((LA, AY, LN), F32), V((NF, AY, LN), F32),
        V((64, 1024), F32), V((CAP, DEV), jnp.int32), V((CAP, DEV), jnp.int32), V((CAP, DEV), jnp.int32),
        V((3, 16, LN), F32), V((1024, LN), F32), V((2, 1024, LN), BF16),
        V((16, LN, LN), BF16), V((16, 256, LN), BF16), V((16, LN, 256), BF16),
        V((CHUNKS, LN, LN), BF16),
        V((CHUNKS, 1024, CW), F32), V((CHUNKS, 1024, CW), F32),
        V((4, DEV, 8, LN), F32), V((4, DEV, 8, LN), F32),
        V((2 * UNROLL, 2, B, LN), F32), V((LN, 256), F32), V((LN, 256), BF16),
        V((ADV, 2, 96, LN), F32), V((ADV, 2, 96, LN), F32), V((ADV, 2, OY, LN), F32), V((ADV, 2, 2, OY, LN), F32),
        V((LO, OY, LN), F32), V((LO, OY, LN), F32), V((LO, OY, LN), F32), V((LO, OY, LN), F32), V((LO, OY, LN), F32),
        V((LO, OY, LN), F32), V((2, LO, OY, LN), F32), V((3, OY, LN), F32), V((LA, AY, LN), F32), V((LA, AY, LN), F32),
        V((PL, OY, LN), F32),
        pltpu.SemaphoreType.DMA((13,)), pltpu.SemaphoreType.DMA, pltpu.SemaphoreType.DMA((ADV, 4)),
        pltpu.SemaphoreType.DMA((ADV, 4)), pltpu.SemaphoreType.DMA((4,)), pltpu.SemaphoreType.DMA((4, GX)),
    ]
    out_tr, out_air, out_sf = pl.pallas_call(
        kernel,
        out_shape=(
            jax.ShapeDtypeStruct((PL, OY, LN), F32),
            jax.ShapeDtypeStruct((LA, AY, LN), F32),
            jax.ShapeDtypeStruct((NF, AY, LN), F32),
        ),
        in_specs=[anyspace] * 12,
        out_specs=(anyspace, vm, vm),
        scratch_shapes=scratch,
        compiler_params=pltpu.CompilerParams(
            collective_id=0, has_side_effects=True, vmem_limit_bytes=60 * 1024 * 1024),
        name="coupling_step",
    )(
        tracers, east_flow, north_flow, ocean_kappa, land_sea, air_temp, air_kappa, air_fluxes,
        weight_tiles, *(jnp.swapaxes(x, 1, 2) for x in (tile_index, send_blocks, receive_blocks)),
    )
    out_tr, out_air, out_sf = pl.pallas_call(
        hand_on,
        out_shape=(
            jax.ShapeDtypeStruct((PL, OY, LN), F32),
            jax.ShapeDtypeStruct((LA, AY, LN), F32),
            jax.ShapeDtypeStruct((NF, AY, LN), F32),
        ),
        in_specs=[anyspace] * 3,
        out_specs=[anyspace] * 3,
        scratch_shapes=[
            V((PL, OY, LN), F32), V((LA, AY, LN), F32), V((NF, AY, LN), F32),
            pltpu.SemaphoreType.DMA((PARTS + 2,)), pltpu.SemaphoreType.DMA((PARTS + 2,)),
        ],
        compiler_params=pltpu.CompilerParams(vmem_limit_bytes=60 * 1024 * 1024),
        name="hand_on",
    )(out_tr, out_air, out_sf)
    return out_tr.reshape(2, LO, OY, LN), out_air, out_sf


def solution(mesh):
    return jax.shard_map(
        shards,
        mesh=mesh,
        in_specs=(
            P(None, None, "gy", "gx"),
            P(None, "gy", "gx"),
            P(None, "gy", "gx"),
            P(None, "gy", "gx"),
            P("gy", "gx"),
            P(None, "gy", "gx"),
            P(None, "gy", "gx"),
            P(None, "gy", "gx"),
            P(("gx", "gy"), None, None),
            P(("gx", "gy"), None, None),
            P(("gx", "gy"), None, None),
            P(("gx", "gy"), None, None),
        ),
        out_specs=(P(None, None, "gy", "gx"), P(None, "gy", "gx"), P(None, "gy", "gx")),
        check_vma=False,
    )
```

```python
import jax
import jax.numpy as jnp
from jax import lax
from jax.experimental import pallas as pl
from jax.experimental.pallas import tpu as pltpu
from jax.sharding import PartitionSpec as P

F32 = jnp.float32
BF16 = jnp.bfloat16
MESH = pl.DeviceIdType.MESH
NF, B, CAP, ADV = 4, 32, 16, 4
GX, GY = 8, 16
DEV = GX * GY
SLOTS = DEV * CAP
LO, LA, OY, AY, LN = 30, 16, 48, 16, 128
PL = 2 * LO
TOP = 8
CHUNKS, CW = 8, 256
GROUP = 10
SENDS = (4, 4)
PARTS = 6
UNROLL = 2


def iota(shape, dim):
    return lax.broadcasted_iota(jnp.int32, shape, dim)


def split(x):
    hi = x.astype(BF16)
    return hi, (x - hi.astype(F32)).astype(BF16)


def fields_to_blocks(fields, q):
    lane = iota(fields[0].shape, 1) >> 5
    out = jnp.zeros_like(fields[0])
    for f in range(len(fields)):
        moved = pltpu.roll(fields[f], ((f - q) * B) % LN, 1) if f != q else fields[f]
        out = jnp.where(lane == f, moved, out)
    return out


def blocks_to_field(groups, f):
    lane = iota(groups[0].shape, 1) >> 5
    out = jnp.zeros_like(groups[0])
    for q in range(4):
        moved = pltpu.roll(groups[q], ((q - f) * B) % LN, 1) if f != q else groups[q]
        out = jnp.where(lane == q, moved, out)
    return out


def slot_rows(idx):
    lane = iota((CAP, LN), 1)
    spread = 2 * (lane & 7) + (lane >> 6) == iota((CAP, LN), 0)
    tiled = jnp.dot(idx.astype(F32).T.astype(BF16), spread.astype(F32).astype(BF16), preferred_element_type=F32)
    own = ((iota((DEV, LN), 1) >> 3) & 7) == (iota((DEV, LN), 0) & 7)
    return jnp.sum(jnp.where(own, tiled, 0.0).reshape(16, 8, LN), axis=1)


def mix_halves(a, b):
    low = iota(a.shape, 1) < 64
    return jnp.where(low, a, pltpu.roll(b, 64, 1)), jnp.where(low, pltpu.roll(a, 64, 1), b)


def pack(a, b):
    return jnp.concatenate(mix_halves(a, b), axis=0).T


def unpack(rows):
    turned = rows.T
    return mix_halves(turned[:64], turned[64:])


def kernel(
    tr, ue, un, kap, land, atemp, akap, aflux, wts, tix, sbl, rbl,
    out_tr, out_air, out_sf,
    va, vb, xs, w_shift, w_edge, u, n, kv, land_v, sea_p, at_v, ak_v, af_v, w_v, ti_v, sb_v, rb_v,
    rows3, w2t, w2p, oh_t, oh_h, oh_ht, oh_b, g1, g2,
    box1_out, box1_in, box_out, box_in, xt, total, st,
    rsend, rrecv, csend, crecv,
    c0, ce, cw, cn, cs, elim_r, elim_z, top_y, air_r, air_z, x_out,
    in_sem, out_sem, hs_sem, hr_sem, as_sem, ar_sem,
):
    gx = lax.axis_index("gx")
    gy = lax.axis_index("gy")
    me = gx * GY + gy

    pairs = (
        (aflux, af_v), (rbl.at[0], rb_v), (land, land_v), (tr.at[0], va.at[:, 0, TOP:TOP + OY, :]), (ue, u), (un, n),
        (wts.at[0], w_v), (tix.at[0], ti_v), (sbl.at[0], sb_v), (kap, kv), (atemp, at_v), (akap, ak_v),
        (tr.at[1], va.at[:, 1, TOP:TOP + OY, :]),
    )
    loads = [pltpu.make_async_copy(s, d, in_sem.at[i]) for i, (s, d) in enumerate(pairs)]
    for c in loads:
        c.start()

    barrier = pltpu.get_barrier_semaphore()

    columns = [lax.rem(gx + i, GX) for i in range(GX)]
    rows = [lax.rem(gy + j, GY) for j in range(GY)]
    for i in range(1, DEV):
        pl.semaphore_signal(
            barrier, inc=1, device_id=(columns[i // GY], rows[i % GY]), device_id_type=MESH)

    lane48 = iota((OY, LN), 1)
    row48 = iota((OY, LN), 0)

    loads[0].wait()
    loads[1].wait()
    tgt = rb_v[...]
    tgt = jnp.where(tgt < 64, (tgt & 3) * AY + (tgt >> 2), -1)
    rows3[1] = slot_rows(tgt)
    air = [af_v[f] for f in range(NF)]
    blocks = jnp.concatenate([fields_to_blocks(air, q) for q in range(4)], axis=0)
    bhi, blo = split(blocks)
    blocks2 = jnp.concatenate([bhi.astype(F32), blo.astype(F32)], axis=0).T.astype(BF16)
    sub128 = iota((LN, LN), 0)

    def pick(c, carry):
        hot = [jnp.where((sub128 & 63).astype(F32) == rows3[1, pl.ds(2 * c + h, 1), :], 1.0, 0.0) for h in range(2)]
        oh_b[c] = jnp.concatenate(mix_halves(hot[0][:64], hot[1][:64]), axis=0).astype(BF16)
        picked = jnp.dot(blocks2, jnp.concatenate(hot, axis=1).astype(BF16), preferred_element_type=F32)
        a, b = picked[:, :LN], picked[:, LN:]
        box1_out[pl.ds(c * 16, 16), 0:8, :] = pack(a[64:], b[64:]).reshape(16, 8, LN)
        box1_out[pl.ds(c * 16, 16), 8:16, :] = pack(a[:64], b[:64]).reshape(16, 8, LN)
        return carry

    lax.fori_loop(0, CHUNKS, pick, 0)
    box1_in[me] = box1_out[me]

    for i in (2, 3, 4, 5, 12):
        loads[i].wait()
    sea = land_v[...].astype(F32)
    sea_p[TOP:TOP + OY, :] = sea

    src, dst = iota((256, 256), 0) & (LN - 1), iota((256, 256), 1)
    to_east = (src == dst + 1) & (dst < LN - 1)
    to_west = (src == dst - 1 - LN) & (dst > LN)
    w_shift[0:256, :] = jnp.where(to_east | to_west, 1.0, 0.0).astype(BF16)
    even = (src & 1) == 0
    w_shift[256:512, :] = jnp.where((even & (dst == LN - 1)) | ((src & 1 == 1) & (dst == LN)), 1.0, 0.0).astype(BF16)
    src, dst = iota((256, LN), 0) & (LN - 1), iota((256, LN), 1)
    even = (dst & 1) == 0
    w_edge[...] = jnp.where((even & (src == LN - 1)) | ((dst & 1 == 1) & (src == 0)), 1.0, 0.0).astype(BF16)

    def keep(p, x):
        xs[pl.ds(pl.multiple_of(p * OY, OY), OY), :] = jnp.concatenate(split(x), axis=1)

    def group_rows(i):
        return pl.ds(pl.multiple_of(i * (2 * GROUP * OY), 2 * GROUP * OY), 2 * GROUP * OY)

    def edge_columns():
        acc = jnp.zeros((OY, LN), F32)
        for i in range(LO // GROUP):
            found = jnp.dot(xs[group_rows(i), :], w_edge[...], preferred_element_type=F32)
            for k in range(2 * GROUP):
                acc = jnp.where((lane48 >> 1) == i * 2 * GROUP + k, found[k * OY:(k + 1) * OY], acc)
        return acc

    def first_edges(i, accu):
        for j in range(GROUP):
            l = i * GROUP + j
            for t in range(2):
                p = 2 * l + t
                x = va[l, t, TOP:TOP + OY, :]
                keep(p, x)
                rsend[0, 0, pl.ds(p, 1), :] = x[OY - 1:OY]
                rsend[0, 1, pl.ds(p, 1), :] = x[0:1]
            accu = jnp.where(lane48 == l, pltpu.roll(u[l] * sea, l + 1, 1), accu)
            rsend[0, 0, pl.ds(PL + l, 1), :] = n[l, OY - 1:OY, :] * sea[OY - 1:OY]
        return accu

    zero48 = jnp.zeros((OY, LN), F32)
    accu = lax.fori_loop(0, LO // GROUP, first_edges, zero48)
    acc = edge_columns()
    acc = jnp.where((lane48 >> 1) == PL, pltpu.roll(sea, 2 * PL + 1, 1), acc)
    csend[0, 0] = acc
    csend[0, 1] = accu
    rsend[0, 1, PL:96, :] = jnp.zeros((96 - PL, LN), F32)
    tail = jnp.where(iota((8, LN), 0) == 2, sea[OY - 1:OY], 0.0)
    rsend[0, 0, 88:96, :] = jnp.where(iota((8, LN), 0) < 2, rsend[0, 0, 88:96, :], tail)
    rsend[0, 1, 88:96, :] = jnp.where(iota((8, LN), 0) == 2, sea[0:1], 0.0)

    @pl.when(gy == 0)
    def _():
        for s in range(ADV):
            rrecv[s, 1] = jnp.zeros((96, LN), F32)

    pl.semaphore_wait(barrier, DEV - 1)

    east, west = lax.rem(gx + 1, GX), lax.rem(gx + GX - 1, GX)

    def lines(s):
        return 96 if s == 0 else 64

    def sides(s):
        return 2 if s == 0 else 1

    def row_copy(s, out, into, to):
        return pltpu.make_async_remote_copy(
            src_ref=rsend.at[s, out, 0:lines(s), :], dst_ref=rrecv.at[s, into, 0:lines(s), :],
            send_sem=hs_sem.at[s, out], recv_sem=hr_sem.at[s, into], device_id=to, device_id_type=MESH)

    def col_copy(s, out, into, to):
        return pltpu.make_async_remote_copy(
            src_ref=csend.at[s, 0:sides(s)], dst_ref=crecv.at[s, into, 0:sides(s)],
            send_sem=hs_sem.at[s, 2 + out], recv_sem=hr_sem.at[s, 2 + into], device_id=to, device_id_type=MESH)

    def send_edges(s):
        col_copy(s, 0, 0, (east, gy)).start()
        col_copy(s, 1, 1, (west, gy)).start()

        @pl.when(gy < GY - 1)
        def _():
            row_copy(s, 0, 1, (gx, gy + 1)).start()

        @pl.when(gy == GY - 1)
        def _():
            row_copy(s, 0, 0, (GX - 1 - gx, gy)).start()

        @pl.when(gy > 0)
        def _():
            row_copy(s, 1, 0, (gx, gy - 1)).start()

    flip = jnp.where(iota((LN, LN), 0) + iota((LN, LN), 1) == LN - 1, 1.0, 0.0)

    def await_edges(s):
        col_copy(s, 0, 0, (east, gy)).wait()
        col_copy(s, 1, 1, (west, gy)).wait()
        row_copy(s, 0, 0, (east, gy)).wait()

        @pl.when(gy > 0)
        def _():
            row_copy(s, 1, 1, (east, gy)).wait()

        @pl.when(gy == GY - 1)
        def _():
            rows = rrecv[s, 0, 0:lines(s), :]
            rrecv[s, 0, 0:lines(s), :] = jnp.dot(
                rows, flip, precision=lax.Precision.HIGHEST, preferred_element_type=F32)

    send_edges(0)

    outs = (box1_out, box_out.at[0], box_out.at[1])
    ins = (box1_in, box_in.at[0], box_in.at[1])

    def send_chunk(k, c, start):
        for py in rows[start:]:
            pltpu.make_async_remote_copy(
                src_ref=outs[k].at[c * GY + py], dst_ref=ins[k].at[me], send_sem=as_sem.at[k],
                recv_sem=ar_sem.at[k, gx], device_id=(c, py), device_id_type=MESH).start()

    def exchange_wait(k, c, blocks):
        return pltpu.make_async_remote_copy(
            src_ref=outs[k].at[pl.ds(0, blocks)], dst_ref=ins[k].at[pl.ds(0, blocks)],
            send_sem=as_sem.at[k], recv_sem=ar_sem.at[k, c], device_id=(east, gy), device_id_type=MESH)

    def chunk_order(i):
        return lax.rem(gx + 1 + i, GX)

    def await_chunk(k, i):
        c = lax.rem(gx + GX - 1 - i, GX)

        @pl.when(i < GX - 1)
        def _():
            exchange_wait(k, c, GY).wait_recv()

        @pl.when(i == GX - 1)
        def _():
            exchange_wait(k, c, GY - 1).wait_recv()

        return c

    def exchange_part(k, begin, end):
        def out(i, carry):
            send_chunk(k, chunk_order(i), 0)
            return carry

        if begin < min(end, GX - 1):
            lax.fori_loop(begin, min(end, GX - 1), out, 0)
        if begin < end == GX:
            send_chunk(k, gx, 1)

    exchange_part(0, 0, SENDS[0])

    for i in (6, 7, 8):
        loads[i].wait()
    rows3[0] = slot_rows(ti_v[...])
    snd = sb_v[...]
    rows3[2] = slot_rows(jnp.where(snd < 192, (snd & 3) * OY + (snd >> 2), -1))
    for c in range(8):
        whi, wlo = split(w_v[:, c * LN:(c + 1) * LN])
        both = jnp.concatenate([whi.astype(F32), wlo.astype(F32)], axis=0)
        w2t[c * LN:(c + 1) * LN, :] = both.T
    w2p[0] = w2t[...].astype(BF16)
    for b in range(B):
        w2p[1, b * B:(b + 1) * B, :] = w2t[pl.ds(b, B, stride=B), :].astype(BF16)

    def hots(g, carry):
        rt = rows3[0, pl.ds(g, 1), :]
        oh_t[g] = jnp.where((sub128 & 63).astype(F32) == rt, 1.0, 0.0).astype(BF16)
        rs = rows3[2, pl.ds(g, 1), :]
        hot = jnp.where(iota((256, LN), 0).astype(F32) == rs, 1.0, 0.0)
        oh_h[g] = hot.astype(BF16)
        oh_ht[g, :, 0:LN] = hot[:LN].T.astype(BF16)
        oh_ht[g, :, LN:] = hot[LN:].T.astype(BF16)
        return carry

    lax.fori_loop(0, 16, hots, 0)

    def tiles(which, out):
        def one(c, carry):
            hot = jnp.concatenate([oh_t[2 * c], oh_t[2 * c + 1]], axis=1)
            out[c] = jnp.dot(w2p[which], hot, preferred_element_type=F32)
            return carry

        lax.fori_loop(0, CHUNKS, one, 0)

    tiles(0, g1)

    await_edges(0)


    def ghosts(s):
        even = (lane48 & 1) == 0
        return jnp.where(even, pltpu.roll(crecv[s, 1, 0], LN - 1, 1), pltpu.roll(crecv[s, 0, 0], 1, 1))

    gh = ghosts(0)
    last = lane48 == LN - 1
    first = lane48 == 0
    gsea = pltpu.roll(gh, LN - 1 - 2 * PL, 1)
    sea_e = jnp.where(last, gsea, pltpu.roll(sea, LN - 1, 1))
    sea_p[TOP + OY:TOP + OY + 1, :] = rrecv[0, 0, 90:91, :]
    sea_n = sea_p[TOP + 1:TOP + 1 + OY, :]
    open_e = sea * sea_e
    open_n = sea * sea_n
    uw_ghost = crecv[0, 0, 1] * jnp.broadcast_to(sea[:, 0:1], (OY, LN))

    def faces(i, carry):
        for j in range(GROUP):
            face(i * GROUP + j)
        return carry

    def face(l):
        um = u[l] * open_e
        uw = jnp.where(first, pltpu.roll(uw_ghost, lax.rem(LN - l, LN), 1), pltpu.roll(um, 1, 1))
        nm = n[l] * open_n
        below = rrecv[0, 1, pl.ds(PL + l, 1), :] * sea[0:1]
        ns = jnp.where(row48 == 0, below, pltpu.roll(nm, 1, 0))
        ce[l] = -jnp.minimum(um, 0.0)
        cw[l] = jnp.maximum(uw, 0.0)
        cn[l] = -jnp.minimum(nm, 0.0)
        cs[l] = jnp.maximum(ns, 0.0)
        c0[l] = 1.0 - jnp.maximum(um, 0.0) + jnp.minimum(uw, 0.0) - jnp.maximum(nm, 0.0) + jnp.minimum(ns, 0.0)

    lax.fori_loop(0, LO // GROUP, faces, 0)

    def apply_tiles(tile_ref, c, h, slot, count):
        out = jnp.zeros((count, B, LN), F32)
        for a in range(B):
            w = tile_ref[c, a * B:(a + 1) * B, h * LN:(h + 1) * LN]
            out = out + w[None] * xt[slot, 0:count, a:a + 1, :]
        return out.reshape(count * B, LN)

    def forcing():
        total[...] = jnp.zeros_like(total)

        def arrive(i, carry):
            await_chunk(0, i)
            return carry

        lax.fori_loop(0, CHUNKS, arrive, 0)

        def spread(i, carry):
            for d in range(UNROLL):
                c = i * UNROLL + d
                for e in range(2):
                    rows = box1_in[pl.ds(c * 16, 16), 8 * e:8 * e + 8, :].reshape(LN, LN)
                    for h, x in enumerate(unpack(rows)):
                        xt[2 * d + h, 2 * e:2 * e + 2] = x.reshape(2, B, LN)
            parts = []
            for d in range(UNROLL):
                c = i * UNROLL + d
                for h in range(2):
                    parts.append(jnp.concatenate(split(apply_tiles(g1, c, h, 2 * d + h, NF)), axis=0))
            total[...] += jnp.dot(
                jnp.concatenate(parts, axis=1), oh_ht[pl.ds(2 * UNROLL * i, 2 * UNROLL)].reshape(UNROLL * CW, 256),
                preferred_element_type=F32)
            return carry

        lax.fori_loop(0, CHUNKS // UNROLL, spread, 0)
        both = total[0:LN, :] + total[LN:, :]
        landed = jnp.concatenate([both[:, :LN].T, both[:, LN:].T], axis=0)
        groups = [landed[q * OY:(q + 1) * OY] for q in range(4)]
        return [blocks_to_field(groups, f) for f in range(NF)]

    def lift(surf):
        sblocks = jnp.concatenate([fields_to_blocks(surf, q) for q in range(4)] + [jnp.zeros((64, LN), F32)], axis=0)
        lifted = jnp.concatenate([sblocks[:LN].T[:64], sblocks[LN:].T[:64]], axis=1)
        st[...] = jnp.concatenate(split(lifted), axis=0)

    def send_terms(e):
        k = 1 + e

        def push(i, carry):
            chunks = [chunk_order(i * UNROLL + d) for d in range(UNROLL)]
            for d, c in enumerate(chunks):
                for h in range(2):
                    two = jnp.dot(st[...], oh_h[2 * c + h], preferred_element_type=F32)
                    xt[2 * d + h, 0:2] = (two[:64] + two[64:]).reshape(2, B, LN)
            for d, c in enumerate(chunks):
                parts = [apply_tiles(g2, c, h, 2 * d + h, 2) for h in range(2)]
                box_out[e, pl.ds(c * 16, 16)] = pack(*parts).reshape(16, 8, LN)
            for d, c in enumerate(chunks):
                if d < UNROLL - 1:
                    send_chunk(k, c, 0)
                    continue

                @pl.when(i < GX // UNROLL - 1)
                def _():
                    send_chunk(k, c, 0)

                @pl.when(i == GX // UNROLL - 1)
                def _():
                    send_chunk(k, c, 1)

            return carry

        lax.fori_loop(0, GX // UNROLL, push, 0)
        box_in[e, me] = box_out[e, me]

    def gather(e):
        def add(i, carry):
            c = await_chunk(1 + e, i)
            rows = box_in[e, pl.ds(c * 16, 16)].reshape(LN, LN)
            return carry + jnp.dot(oh_b[c], jnp.concatenate(split(rows), axis=1), preferred_element_type=F32)

        both = lax.fori_loop(0, GX, add, jnp.zeros((LN, 256), F32))
        both = both[:, :LN] + both[:, LN:]
        landed = both[:64] + pltpu.roll(both[64:], 64, 1)
        groups = [landed[q * AY:(q + 1) * AY] for q in range(4)]
        return [blocks_to_field(groups, f) for f in range(2)]

    def before_wait(s):
        if s == 1:
            tiles(1, g2)
        if s == 2:
            f2, f3, f0, f1 = forcing()
            top_y[3], top_y[4] = f0, f1
            lift([sea * (u[0] + 0.1 * jnp.tanh(f2)), sea * (n[0] + 0.1 * jnp.tanh(f3))])
        if s == 3:
            send_terms(0)

    for s in range(ADV):
        if s > 0:
            before_wait(s)
            await_edges(s)
        gh = ghosts(s)
        now, later = (va, vb) if s % 2 == 0 else (vb, va)

        def edges_in(i, carry, s=s, now=now):
            for j in range(GROUP):
                l = i * GROUP + j
                for t in range(2):
                    now[l, t, TOP - 1:TOP, :] = rrecv[s, 1, pl.ds(2 * l + t, 1), :]
                    now[l, t, TOP + OY:TOP + OY + 1, :] = rrecv[s, 0, pl.ds(2 * l + t, 1), :]
            return carry

        lax.fori_loop(0, LO // GROUP, edges_in, 0)
        ghi, glo = (x.astype(F32) for x in split(gh))

        def substep(i, carry, s=s, now=now, later=later, ghi=ghi, glo=glo):
            parts = []
            for k in range(2 * GROUP):
                own = (lane48 >> 1) == i * 2 * GROUP + k
                parts.append(jnp.concatenate(
                    [jnp.where(own, ghi, 0.0).astype(BF16), jnp.where(own, glo, 0.0).astype(BF16)], axis=1))
            near = jnp.dot(
                jnp.concatenate([xs[group_rows(i), :], jnp.concatenate(parts, axis=0)], axis=1), w_shift[...],
                preferred_element_type=F32)
            for j in range(GROUP):
                l = i * GROUP + j
                k0, ke, kw, kn, ks = c0[l], ce[l], cw[l], cn[l], cs[l]
                for t in range(2):
                    k = 2 * j + t
                    rows = near[k * OY:(k + 1) * OY]
                    y = k0 * now[l, t, TOP:TOP + OY, :] + ke * rows[:, :LN] + kw * rows[:, LN:]
                    y = y + kn * now[l, t, TOP + 1:TOP + 1 + OY, :] + ks * now[l, t, TOP - 1:TOP - 1 + OY, :]
                    later[l, t, TOP:TOP + OY, :] = y
                    if s < ADV - 1:
                        p = 2 * l + t
                        keep(p, y)
                        rsend[s + 1, 0, pl.ds(p, 1), :] = y[OY - 1:OY]
                        rsend[s + 1, 1, pl.ds(p, 1), :] = y[0:1]
            return carry

        lax.fori_loop(0, LO // GROUP, substep, 0)
        if s < ADV - 1:
            csend[s + 1, 0] = edge_columns()
            for k in range(2):
                rsend[s + 1, k, PL:64, :] = jnp.zeros((64 - PL, LN), F32)
            send_edges(s + 1)
            if s + 1 < len(SENDS):
                exchange_part(0, sum(SENDS[:s + 1]), sum(SENDS[:s + 2]))

    loads[9].wait()

    def up(i, carry):
        e, yt, ys = carry
        l = LO - 2 - i
        k = kv[l] * sea
        inv = 1.0 / (e + k)
        r = k * inv
        elim_r[l + 1] = r
        elim_z[0, l + 1] = yt * inv
        elim_z[1, l + 1] = ys * inv
        return (1.0 + k * (1.0 - r), va[l, 0, TOP:TOP + OY, :] + r * yt, va[l, 1, TOP:TOP + OY, :] + r * ys)

    start = (jnp.ones((OY, LN), F32), va[LO - 1, 0, TOP:TOP + OY, :], va[LO - 1, 1, TOP:TOP + OY, :])
    e, yt, ys = lax.fori_loop(0, LO - 1, up, start)
    inv = 1.0 / e
    top_y[0], top_y[1], top_y[2] = yt, ys, inv

    loads[10].wait()
    loads[11].wait()

    def air_up(i, carry):
        e, y = carry
        l = LA - 2 - i
        k = ak_v[l + 1]
        inv = 1.0 / (e + k)
        r = k * inv
        air_r[l + 1] = r
        air_z[l + 1] = y * inv
        return 1.0 + k * (1.0 - r), at_v[l] + r * y

    ea, ya = lax.fori_loop(0, LA - 1, air_up, (jnp.ones((AY, LN), F32), at_v[LA - 1]))
    inv_a = 1.0 / (ea + ak_v[0])
    air_z[0] = ya
    air_r[0] = inv_a

    xt0 = (top_y[0] + sea * top_y[3]) * top_y[2]
    xs0 = (top_y[1] + sea * top_y[4]) * top_y[2]
    lift([sea * xt0, sea])
    send_terms(1)

    x_out[0] = xt0
    x_out[LO] = xs0

    def down(l, carry):
        a, b = carry
        r = elim_r[l]
        a = elim_z[0, l] + r * a
        b = elim_z[1, l] + r * b
        x_out[l] = a
        x_out[LO + l] = b
        return a, b

    lax.fori_loop(1, LO, down, (xt0, xs0))
    store = pltpu.make_async_copy(x_out, out_tr, out_sem)
    store.start()

    late = gather(0)
    fields = gather(1) + late
    for f in range(NF):
        out_sf[f] = fields[f]
    ground = at_v[0] * (1.0 - fields[1]) + fields[0]
    x = (air_z[0] + ak_v[0] * ground) * air_r[0]
    out_air[0] = x
    for l in range(1, LA):
        x = air_z[l] + air_r[l] * x
        out_air[l] = x

    for k in range(3):
        exchange_wait(k, gx, DEV - 1).wait_send()
    store.wait()


def hand_on(tr, air, sf, out_tr, out_air, out_sf, tr_v, air_v, sf_v, sem_in, sem_out):
    step = PL // PARTS
    parts = [pl.ds(i * step, step) for i in range(PARTS)]
    trios = [(tr.at[p], tr_v.at[p], out_tr.at[p]) for p in parts] + [(air, air_v, out_air), (sf, sf_v, out_sf)]
    ins = [pltpu.make_async_copy(a, b, sem_in.at[i]) for i, (a, b, _) in enumerate(trios)]
    outs = [pltpu.make_async_copy(b, c, sem_out.at[i]) for i, (_, b, c) in enumerate(trios)]
    for copy in ins:
        copy.start()
    for copy, back in zip(ins, outs):
        copy.wait()
        back.start()
    for back in outs:
        back.wait()


def shards(
    tracers, east_flow, north_flow, ocean_kappa, land_sea, air_temp, air_kappa, air_fluxes,
    weight_tiles, tile_index, send_blocks, receive_blocks,
):
    anyspace = pl.BlockSpec(memory_space=pl.ANY)
    vm = pl.BlockSpec(memory_space=pltpu.VMEM)
    V = pltpu.VMEM
    scratch = [
        V((LO, 2, 64, LN), F32), V((LO, 2, 64, LN), F32), V((PL * OY, 256), BF16), V((512, 256), BF16),
        V((256, LN), BF16), V((LO, OY, LN), F32), V((LO, OY, LN), F32), V((LO - 1, OY, LN), F32),
        V((OY, LN), jnp.int32), V((64, LN), F32), V((LA, AY, LN), F32), V((LA, AY, LN), F32), V((NF, AY, LN), F32),
        V((64, 1024), F32), V((CAP, DEV), jnp.int32), V((CAP, DEV), jnp.int32), V((CAP, DEV), jnp.int32),
        V((3, 16, LN), F32), V((1024, LN), F32), V((2, 1024, LN), BF16),
        V((16, LN, LN), BF16), V((16, 256, LN), BF16), V((16, LN, 256), BF16),
        V((CHUNKS, LN, LN), BF16),
        V((CHUNKS, 1024, CW), F32), V((CHUNKS, 1024, CW), F32),
        V((DEV, 16, LN), F32), V((DEV, 16, LN), F32), V((2, DEV, 8, LN), F32), V((2, DEV, 8, LN), F32),
        V((2 * UNROLL, NF, B, LN), F32), V((256, 256), F32), V((LN, 256), BF16),
        V((ADV, 2, 96, LN), F32), V((ADV, 2, 96, LN), F32), V((ADV, 2, OY, LN), F32), V((ADV, 2, 2, OY, LN), F32),
        V((LO, OY, LN), F32), V((LO, OY, LN), F32), V((LO, OY, LN), F32), V((LO, OY, LN), F32), V((LO, OY, LN), F32),
        V((LO, OY, LN), F32), V((2, LO, OY, LN), F32), V((5, OY, LN), F32), V((LA, AY, LN), F32), V((LA, AY, LN), F32),
        V((PL, OY, LN), F32),
        pltpu.SemaphoreType.DMA((13,)), pltpu.SemaphoreType.DMA, pltpu.SemaphoreType.DMA((ADV, 4)),
        pltpu.SemaphoreType.DMA((ADV, 4)), pltpu.SemaphoreType.DMA((3,)), pltpu.SemaphoreType.DMA((3, GX)),
    ]
    out_tr, out_air, out_sf = pl.pallas_call(
        kernel,
        out_shape=(
            jax.ShapeDtypeStruct((PL, OY, LN), F32),
            jax.ShapeDtypeStruct((LA, AY, LN), F32),
            jax.ShapeDtypeStruct((NF, AY, LN), F32),
        ),
        in_specs=[anyspace] * 12,
        out_specs=(anyspace, vm, vm),
        scratch_shapes=scratch,
        compiler_params=pltpu.CompilerParams(
            collective_id=0, has_side_effects=True, vmem_limit_bytes=60 * 1024 * 1024),
        name="coupling_step",
    )(
        tracers, east_flow, north_flow, ocean_kappa, land_sea, air_temp, air_kappa, air_fluxes,
        weight_tiles, *(jnp.swapaxes(x, 1, 2) for x in (tile_index, send_blocks, receive_blocks)),
    )
    out_tr, out_air, out_sf = pl.pallas_call(
        hand_on,
        out_shape=(
            jax.ShapeDtypeStruct((PL, OY, LN), F32),
            jax.ShapeDtypeStruct((LA, AY, LN), F32),
            jax.ShapeDtypeStruct((NF, AY, LN), F32),
        ),
        in_specs=[anyspace] * 3,
        out_specs=[anyspace] * 3,
        scratch_shapes=[
            V((PL, OY, LN), F32), V((LA, AY, LN), F32), V((NF, AY, LN), F32),
            pltpu.SemaphoreType.DMA((PARTS + 2,)), pltpu.SemaphoreType.DMA((PARTS + 2,)),
        ],
        compiler_params=pltpu.CompilerParams(vmem_limit_bytes=60 * 1024 * 1024),
        name="hand_on",
    )(out_tr, out_air, out_sf)
    return out_tr.reshape(2, LO, OY, LN), out_air, out_sf


def solution(mesh):
    return jax.shard_map(
        shards,
        mesh=mesh,
        in_specs=(
            P(None, None, "gy", "gx"),
            P(None, "gy", "gx"),
            P(None, "gy", "gx"),
            P(None, "gy", "gx"),
            P("gy", "gx"),
            P(None, "gy", "gx"),
            P(None, "gy", "gx"),
            P(None, "gy", "gx"),
            P(("gx", "gy"), None, None),
            P(("gx", "gy"), None, None),
            P(("gx", "gy"), None, None),
            P(("gx", "gy"), None, None),
        ),
        out_specs=(P(None, None, "gy", "gx"), P(None, "gy", "gx"), P(None, "gy", "gx")),
        check_vma=False,
    )
```

```python
import jax
import jax.numpy as jnp
from jax import lax
from jax.experimental import pallas as pl
from jax.experimental.pallas import tpu as pltpu
from jax.sharding import PartitionSpec as P

F32 = jnp.float32
BF16 = jnp.bfloat16
MESH = pl.DeviceIdType.MESH
NF, B, CAP, ADV = 4, 32, 16, 4
GX, GY = 8, 16
DEV = GX * GY
SLOTS = DEV * CAP
LO, LA, OY, AY, LN = 30, 16, 48, 16, 128
PL = 2 * LO
TOP = 8
CHUNKS, CW = 8, 256
GROUP = 10
SENDS = (4, 4)
PARTS = 6
UNROLL = 2


def iota(shape, dim):
    return lax.broadcasted_iota(jnp.int32, shape, dim)


def split(x):
    hi = x.astype(BF16)
    return hi, (x - hi.astype(F32)).astype(BF16)


def fields_to_blocks(fields, q):
    lane = iota(fields[0].shape, 1) >> 5
    out = jnp.zeros_like(fields[0])
    for f in range(len(fields)):
        moved = pltpu.roll(fields[f], ((f - q) * B) % LN, 1) if f != q else fields[f]
        out = jnp.where(lane == f, moved, out)
    return out


def blocks_to_field(groups, f):
    lane = iota(groups[0].shape, 1) >> 5
    out = jnp.zeros_like(groups[0])
    for q in range(4):
        moved = pltpu.roll(groups[q], ((q - f) * B) % LN, 1) if f != q else groups[q]
        out = jnp.where(lane == q, moved, out)
    return out


def slot_rows(idx):
    lane = iota((CAP, LN), 1)
    spread = 2 * (lane & 7) + (lane >> 6) == iota((CAP, LN), 0)
    tiled = jnp.dot(idx.astype(F32).T.astype(BF16), spread.astype(F32).astype(BF16), preferred_element_type=F32)
    own = ((iota((DEV, LN), 1) >> 3) & 7) == (iota((DEV, LN), 0) & 7)
    return jnp.sum(jnp.where(own, tiled, 0.0).reshape(16, 8, LN), axis=1)


def mix_halves(a, b):
    low = iota(a.shape, 1) < 64
    return jnp.where(low, a, pltpu.roll(b, 64, 1)), jnp.where(low, pltpu.roll(a, 64, 1), b)


def pack(a, b):
    return jnp.concatenate(mix_halves(a, b), axis=0).T


def unpack(rows):
    turned = rows.T
    return mix_halves(turned[:64], turned[64:])


def kernel(
    tr, ue, un, kap, land, atemp, akap, aflux, wts, tix, sbl, rbl,
    out_tr, out_air, out_sf,
    va, vb, xs, w_shift, w_edge, u, n, kv, land_v, sea_p, at_v, ak_v, af_v, w_v, ti_v, sb_v, rb_v,
    rows3, w2t, w2p, oh_t, oh_h, oh_ht, oh_b, g1, g2,
    box1_out, box1_in, box_out, box_in, xt, total, st,
    rsend, rrecv, csend, crecv,
    c0, ce, cw, cn, cs, elim_r, elim_i, elim_z, top_y, air_r, air_z, x_out,
    in_sem, out_sem, hs_sem, hr_sem, as_sem, ar_sem,
):
    gx = lax.axis_index("gx")
    gy = lax.axis_index("gy")
    me = gx * GY + gy

    pairs = (
        (aflux, af_v), (rbl.at[0], rb_v), (land, land_v), (tr.at[0], va.at[:, 0, TOP:TOP + OY, :]), (ue, u), (un, n),
        (wts.at[0], w_v), (tix.at[0], ti_v), (sbl.at[0], sb_v), (kap, kv), (atemp, at_v), (akap, ak_v),
        (tr.at[1], va.at[:, 1, TOP:TOP + OY, :]),
    )
    loads = [pltpu.make_async_copy(s, d, in_sem.at[i]) for i, (s, d) in enumerate(pairs)]
    for c in loads:
        c.start()

    barrier = pltpu.get_barrier_semaphore()

    columns = [lax.rem(gx + i, GX) for i in range(GX)]
    rows = [lax.rem(gy + j, GY) for j in range(GY)]
    for i in range(1, DEV):
        pl.semaphore_signal(
            barrier, inc=1, device_id=(columns[i // GY], rows[i % GY]), device_id_type=MESH)

    lane48 = iota((OY, LN), 1)
    row48 = iota((OY, LN), 0)

    loads[0].wait()
    loads[1].wait()
    tgt = rb_v[...]
    tgt = jnp.where(tgt < 64, (tgt & 3) * AY + (tgt >> 2), -1)
    rows3[1] = slot_rows(tgt)
    air = [af_v[f] for f in range(NF)]
    blocks = jnp.concatenate([fields_to_blocks(air, q) for q in range(4)], axis=0)
    bhi, blo = split(blocks)
    blocks2 = jnp.concatenate([bhi.astype(F32), blo.astype(F32)], axis=0).T.astype(BF16)
    sub128 = iota((LN, LN), 0)

    def pick(c, carry):
        hot = [jnp.where((sub128 & 63).astype(F32) == rows3[1, pl.ds(2 * c + h, 1), :], 1.0, 0.0) for h in range(2)]
        oh_b[c] = jnp.concatenate(mix_halves(hot[0][:64], hot[1][:64]), axis=0).astype(BF16)
        picked = jnp.dot(blocks2, jnp.concatenate(hot, axis=1).astype(BF16), preferred_element_type=F32)
        a, b = picked[:, :LN], picked[:, LN:]
        box1_out[pl.ds(c * 16, 16), 0:8, :] = pack(a[64:], b[64:]).reshape(16, 8, LN)
        box1_out[pl.ds(c * 16, 16), 8:16, :] = pack(a[:64], b[:64]).reshape(16, 8, LN)
        return carry

    lax.fori_loop(0, CHUNKS, pick, 0)
    box1_in[me] = box1_out[me]

    for i in (2, 3, 4, 5, 12):
        loads[i].wait()
    sea = land_v[...].astype(F32)
    sea_p[TOP:TOP + OY, :] = sea

    src, dst = iota((256, 256), 0) & (LN - 1), iota((256, 256), 1)
    to_east = (src == dst + 1) & (dst < LN - 1)
    to_west = (src == dst - 1 - LN) & (dst > LN)
    w_shift[0:256, :] = jnp.where(to_east | to_west, 1.0, 0.0).astype(BF16)
    even = (src & 1) == 0
    w_shift[256:512, :] = jnp.where((even & (dst == LN - 1)) | ((src & 1 == 1) & (dst == LN)), 1.0, 0.0).astype(BF16)
    src, dst = iota((256, LN), 0) & (LN - 1), iota((256, LN), 1)
    even = (dst & 1) == 0
    w_edge[...] = jnp.where((even & (src == LN - 1)) | ((dst & 1 == 1) & (src == 0)), 1.0, 0.0).astype(BF16)

    def keep(p, x):
        xs[pl.ds(pl.multiple_of(p * OY, OY), OY), :] = jnp.concatenate(split(x), axis=1)

    def group_rows(i):
        return pl.ds(pl.multiple_of(i * (2 * GROUP * OY), 2 * GROUP * OY), 2 * GROUP * OY)

    def edge_columns():
        acc = jnp.zeros((OY, LN), F32)
        for i in range(LO // GROUP):
            found = jnp.dot(xs[group_rows(i), :], w_edge[...], preferred_element_type=F32)
            for k in range(2 * GROUP):
                acc = jnp.where((lane48 >> 1) == i * 2 * GROUP + k, found[k * OY:(k + 1) * OY], acc)
        return acc

    def first_edges(i, accu):
        for j in range(GROUP):
            l = i * GROUP + j
            for t in range(2):
                p = 2 * l + t
                x = va[l, t, TOP:TOP + OY, :]
                keep(p, x)
                rsend[0, 0, pl.ds(p, 1), :] = x[OY - 1:OY]
                rsend[0, 1, pl.ds(p, 1), :] = x[0:1]
            accu = jnp.where(lane48 == l, pltpu.roll(u[l] * sea, l + 1, 1), accu)
            rsend[0, 0, pl.ds(PL + l, 1), :] = n[l, OY - 1:OY, :] * sea[OY - 1:OY]
        return accu

    zero48 = jnp.zeros((OY, LN), F32)
    accu = lax.fori_loop(0, LO // GROUP, first_edges, zero48)
    acc = edge_columns()
    acc = jnp.where((lane48 >> 1) == PL, pltpu.roll(sea, 2 * PL + 1, 1), acc)
    csend[0, 0] = acc
    csend[0, 1] = accu
    rsend[0, 1, PL:96, :] = jnp.zeros((96 - PL, LN), F32)
    tail = jnp.where(iota((8, LN), 0) == 2, sea[OY - 1:OY], 0.0)
    rsend[0, 0, 88:96, :] = jnp.where(iota((8, LN), 0) < 2, rsend[0, 0, 88:96, :], tail)
    rsend[0, 1, 88:96, :] = jnp.where(iota((8, LN), 0) == 2, sea[0:1], 0.0)

    @pl.when(gy == 0)
    def _():
        for s in range(ADV):
            rrecv[s, 1] = jnp.zeros((96, LN), F32)

    pl.semaphore_wait(barrier, DEV - 1)

    east, west = lax.rem(gx + 1, GX), lax.rem(gx + GX - 1, GX)

    def lines(s):
        return 96 if s == 0 else 64

    def sides(s):
        return 2 if s == 0 else 1

    def row_copy(s, out, into, to):
        return pltpu.make_async_remote_copy(
            src_ref=rsend.at[s, out, 0:lines(s), :], dst_ref=rrecv.at[s, into, 0:lines(s), :],
            send_sem=hs_sem.at[s, out], recv_sem=hr_sem.at[s, into], device_id=to, device_id_type=MESH)

    def col_copy(s, out, into, to):
        return pltpu.make_async_remote_copy(
            src_ref=csend.at[s, 0:sides(s)], dst_ref=crecv.at[s, into, 0:sides(s)],
            send_sem=hs_sem.at[s, 2 + out], recv_sem=hr_sem.at[s, 2 + into], device_id=to, device_id_type=MESH)

    def send_edges(s):
        col_copy(s, 0, 0, (east, gy)).start()
        col_copy(s, 1, 1, (west, gy)).start()

        @pl.when(gy < GY - 1)
        def _():
            row_copy(s, 0, 1, (gx, gy + 1)).start()

        @pl.when(gy == GY - 1)
        def _():
            row_copy(s, 0, 0, (GX - 1 - gx, gy)).start()

        @pl.when(gy > 0)
        def _():
            row_copy(s, 1, 0, (gx, gy - 1)).start()

    flip = jnp.where(iota((LN, LN), 0) + iota((LN, LN), 1) == LN - 1, 1.0, 0.0)

    def await_edges(s):
        col_copy(s, 0, 0, (east, gy)).wait()
        col_copy(s, 1, 1, (west, gy)).wait()
        row_copy(s, 0, 0, (east, gy)).wait()

        @pl.when(gy > 0)
        def _():
            row_copy(s, 1, 1, (east, gy)).wait()

        @pl.when(gy == GY - 1)
        def _():
            rows = rrecv[s, 0, 0:lines(s), :]
            rrecv[s, 0, 0:lines(s), :] = jnp.dot(
                rows, flip, precision=lax.Precision.HIGHEST, preferred_element_type=F32)

    send_edges(0)

    outs = (box1_out, box_out.at[0], box_out.at[1])
    ins = (box1_in, box_in.at[0], box_in.at[1])

    def send_chunk(k, c, start):
        for py in rows[start:]:
            pltpu.make_async_remote_copy(
                src_ref=outs[k].at[c * GY + py], dst_ref=ins[k].at[me], send_sem=as_sem.at[k],
                recv_sem=ar_sem.at[k, gx], device_id=(c, py), device_id_type=MESH).start()

    def exchange_wait(k, c, blocks):
        return pltpu.make_async_remote_copy(
            src_ref=outs[k].at[pl.ds(0, blocks)], dst_ref=ins[k].at[pl.ds(0, blocks)],
            send_sem=as_sem.at[k], recv_sem=ar_sem.at[k, c], device_id=(east, gy), device_id_type=MESH)

    def chunk_order(i):
        return lax.rem(gx + 1 + i, GX)

    def await_chunk(k, i):
        c = lax.rem(gx + GX - 1 - i, GX)

        @pl.when(i < GX - 1)
        def _():
            exchange_wait(k, c, GY).wait_recv()

        @pl.when(i == GX - 1)
        def _():
            exchange_wait(k, c, GY - 1).wait_recv()

        return c

    def exchange_part(k, begin, end):
        def out(i, carry):
            send_chunk(k, chunk_order(i), 0)
            return carry

        if begin < min(end, GX - 1):
            lax.fori_loop(begin, min(end, GX - 1), out, 0)
        if begin < end == GX:
            send_chunk(k, gx, 1)

    exchange_part(0, 0, SENDS[0])

    for i in (6, 7, 8):
        loads[i].wait()
    rows3[0] = slot_rows(ti_v[...])
    snd = sb_v[...]
    rows3[2] = slot_rows(jnp.where(snd < 192, (snd & 3) * OY + (snd >> 2), -1))
    for c in range(8):
        whi, wlo = split(w_v[:, c * LN:(c + 1) * LN])
        both = jnp.concatenate([whi.astype(F32), wlo.astype(F32)], axis=0)
        w2t[c * LN:(c + 1) * LN, :] = both.T
    w2p[0] = w2t[...].astype(BF16)
    for b in range(B):
        w2p[1, b * B:(b + 1) * B, :] = w2t[pl.ds(b, B, stride=B), :].astype(BF16)

    def hots(g, carry):
        rt = rows3[0, pl.ds(g, 1), :]
        oh_t[g] = jnp.where((sub128 & 63).astype(F32) == rt, 1.0, 0.0).astype(BF16)
        rs = rows3[2, pl.ds(g, 1), :]
        hot = jnp.where(iota((256, LN), 0).astype(F32) == rs, 1.0, 0.0)
        oh_h[g] = hot.astype(BF16)
        oh_ht[g, :, 0:LN] = hot[:LN].T.astype(BF16)
        oh_ht[g, :, LN:] = hot[LN:].T.astype(BF16)
        return carry

    lax.fori_loop(0, 16, hots, 0)

    def tiles(which, out):
        def one(c, carry):
            hot = jnp.concatenate([oh_t[2 * c], oh_t[2 * c + 1]], axis=1)
            out[c] = jnp.dot(w2p[which], hot, preferred_element_type=F32)
            return carry

        lax.fori_loop(0, CHUNKS, one, 0)

    tiles(0, g1)

    await_edges(0)


    def ghosts(s):
        even = (lane48 & 1) == 0
        return jnp.where(even, pltpu.roll(crecv[s, 1, 0], LN - 1, 1), pltpu.roll(crecv[s, 0, 0], 1, 1))

    gh = ghosts(0)
    last = lane48 == LN - 1
    first = lane48 == 0
    gsea = pltpu.roll(gh, LN - 1 - 2 * PL, 1)
    sea_e = jnp.where(last, gsea, pltpu.roll(sea, LN - 1, 1))
    sea_p[TOP + OY:TOP + OY + 1, :] = rrecv[0, 0, 90:91, :]
    sea_n = sea_p[TOP + 1:TOP + 1 + OY, :]
    open_e = sea * sea_e
    open_n = sea * sea_n
    uw_ghost = crecv[0, 0, 1] * jnp.broadcast_to(sea[:, 0:1], (OY, LN))

    def faces(i, carry):
        for j in range(GROUP):
            face(i * GROUP + j)
        return carry

    def face(l):
        um = u[l] * open_e
        uw = jnp.where(first, pltpu.roll(uw_ghost, lax.rem(LN - l, LN), 1), pltpu.roll(um, 1, 1))
        nm = n[l] * open_n
        below = rrecv[0, 1, pl.ds(PL + l, 1), :] * sea[0:1]
        ns = jnp.where(row48 == 0, below, pltpu.roll(nm, 1, 0))
        ce[l] = -jnp.minimum(um, 0.0)
        cw[l] = jnp.maximum(uw, 0.0)
        cn[l] = -jnp.minimum(nm, 0.0)
        cs[l] = jnp.maximum(ns, 0.0)
        c0[l] = 1.0 - jnp.maximum(um, 0.0) + jnp.minimum(uw, 0.0) - jnp.maximum(nm, 0.0) + jnp.minimum(ns, 0.0)

    lax.fori_loop(0, LO // GROUP, faces, 0)

    def apply_tiles(tile_ref, c, h, slot, count):
        out = jnp.zeros((count, B, LN), F32)
        for a in range(B):
            w = tile_ref[c, a * B:(a + 1) * B, h * LN:(h + 1) * LN]
            out = out + w[None] * xt[slot, 0:count, a:a + 1, :]
        return out.reshape(count * B, LN)

    def forcing():
        total[...] = jnp.zeros_like(total)

        def arrive(i, carry):
            await_chunk(0, i)
            return carry

        lax.fori_loop(0, CHUNKS, arrive, 0)

        def spread(i, carry):
            for d in range(UNROLL):
                c = i * UNROLL + d
                for e in range(2):
                    rows = box1_in[pl.ds(c * 16, 16), 8 * e:8 * e + 8, :].reshape(LN, LN)
                    for h, x in enumerate(unpack(rows)):
                        xt[2 * d + h, 2 * e:2 * e + 2] = x.reshape(2, B, LN)
            parts = []
            for d in range(UNROLL):
                c = i * UNROLL + d
                for h in range(2):
                    parts.append(jnp.concatenate(split(apply_tiles(g1, c, h, 2 * d + h, NF)), axis=0))
            total[...] += jnp.dot(
                jnp.concatenate(parts, axis=1), oh_ht[pl.ds(2 * UNROLL * i, 2 * UNROLL)].reshape(UNROLL * CW, 256),
                preferred_element_type=F32)
            return carry

        lax.fori_loop(0, CHUNKS // UNROLL, spread, 0)
        both = total[0:LN, :] + total[LN:, :]
        landed = jnp.concatenate([both[:, :LN].T, both[:, LN:].T], axis=0)
        groups = [landed[q * OY:(q + 1) * OY] for q in range(4)]
        return [blocks_to_field(groups, f) for f in range(NF)]

    def lift(surf):
        sblocks = jnp.concatenate([fields_to_blocks(surf, q) for q in range(4)] + [jnp.zeros((64, LN), F32)], axis=0)
        lifted = jnp.concatenate([sblocks[:LN].T[:64], sblocks[LN:].T[:64]], axis=1)
        st[...] = jnp.concatenate(split(lifted), axis=0)

    def send_terms(e):
        k = 1 + e

        def push(i, carry):
            chunks = [chunk_order(i * UNROLL + d) for d in range(UNROLL)]
            for d, c in enumerate(chunks):
                for h in range(2):
                    two = jnp.dot(st[...], oh_h[2 * c + h], preferred_element_type=F32)
                    xt[2 * d + h, 0:2] = (two[:64] + two[64:]).reshape(2, B, LN)
            for d, c in enumerate(chunks):
                parts = [apply_tiles(g2, c, h, 2 * d + h, 2) for h in range(2)]
                box_out[e, pl.ds(c * 16, 16)] = pack(*parts).reshape(16, 8, LN)
            for d, c in enumerate(chunks):
                if d < UNROLL - 1:
                    send_chunk(k, c, 0)
                    continue

                @pl.when(i < GX // UNROLL - 1)
                def _():
                    send_chunk(k, c, 0)

                @pl.when(i == GX // UNROLL - 1)
                def _():
                    send_chunk(k, c, 1)

            return carry

        lax.fori_loop(0, GX // UNROLL, push, 0)
        box_in[e, me] = box_out[e, me]

    def gather(e):
        def add(i, carry):
            c = await_chunk(1 + e, i)
            rows = box_in[e, pl.ds(c * 16, 16)].reshape(LN, LN)
            return carry + jnp.dot(oh_b[c], jnp.concatenate(split(rows), axis=1), preferred_element_type=F32)

        both = lax.fori_loop(0, GX, add, jnp.zeros((LN, 256), F32))
        both = both[:, :LN] + both[:, LN:]
        landed = both[:64] + pltpu.roll(both[64:], 64, 1)
        groups = [landed[q * AY:(q + 1) * AY] for q in range(4)]
        return [blocks_to_field(groups, f) for f in range(2)]

    def before_wait(s):
        if s == 1:
            tiles(1, g2)
        if s == 2:
            f2, f3, f0, f1 = forcing()
            top_y[3], top_y[4] = f0, f1
            lift([sea * (u[0] + 0.1 * jnp.tanh(f2)), sea * (n[0] + 0.1 * jnp.tanh(f3))])
        if s == 3:
            send_terms(0)

    for s in range(ADV):
        if s > 0:
            before_wait(s)
            await_edges(s)
        gh = ghosts(s)
        now, later = (va, vb) if s % 2 == 0 else (vb, va)

        def edges_in(i, carry, s=s, now=now):
            for j in range(GROUP):
                l = i * GROUP + j
                for t in range(2):
                    now[l, t, TOP - 1:TOP, :] = rrecv[s, 1, pl.ds(2 * l + t, 1), :]
                    now[l, t, TOP + OY:TOP + OY + 1, :] = rrecv[s, 0, pl.ds(2 * l + t, 1), :]
            return carry

        lax.fori_loop(0, LO // GROUP, edges_in, 0)
        ghi, glo = (x.astype(F32) for x in split(gh))

        def substep(i, carry, s=s, now=now, later=later, ghi=ghi, glo=glo, tracers=(0, 1)):
            planes = [(i * GROUP + j, t) for j in range(GROUP) for t in tracers]
            parts, lines_here = [], []
            for l, t in planes:
                p = 2 * l + t
                own = (lane48 >> 1) == p
                parts.append(jnp.concatenate(
                    [jnp.where(own, ghi, 0.0).astype(BF16), jnp.where(own, glo, 0.0).astype(BF16)], axis=1))
                lines_here.append(xs[pl.ds(pl.multiple_of(p * OY, OY), OY), :])
            near = jnp.dot(
                jnp.concatenate([jnp.concatenate(lines_here, axis=0), jnp.concatenate(parts, axis=0)], axis=1),
                w_shift[...], preferred_element_type=F32)
            for k, (l, t) in enumerate(planes):
                near_k = near[k * OY:(k + 1) * OY]
                y = c0[l] * now[l, t, TOP:TOP + OY, :] + ce[l] * near_k[:, :LN] + cw[l] * near_k[:, LN:]
                y = y + cn[l] * now[l, t, TOP + 1:TOP + 1 + OY, :] + cs[l] * now[l, t, TOP - 1:TOP - 1 + OY, :]
                later[l, t, TOP:TOP + OY, :] = y
                if s < ADV - 1:
                    p = 2 * l + t
                    keep(p, y)
                    rsend[s + 1, 0, pl.ds(p, 1), :] = y[OY - 1:OY]
                    rsend[s + 1, 1, pl.ds(p, 1), :] = y[0:1]
            return carry

        if s < ADV - 1:
            lax.fori_loop(0, LO // GROUP, substep, 0)
        else:
            lax.fori_loop(0, LO // GROUP, lambda i, carry, f=substep: f(i, carry, tracers=(0,)), 0)
        if s < ADV - 1:
            csend[s + 1, 0] = edge_columns()
            for k in range(2):
                rsend[s + 1, k, PL:64, :] = jnp.zeros((64 - PL, LN), F32)
            send_edges(s + 1)
            if s + 1 < len(SENDS):
                exchange_part(0, sum(SENDS[:s + 1]), sum(SENDS[:s + 2]))

    loads[9].wait()

    def up(i, carry):
        e, yt = carry
        l = LO - 2 - i
        k = kv[l] * sea
        inv = 1.0 / (e + k)
        r = k * inv
        elim_r[l + 1] = r
        elim_i[l + 1] = inv
        elim_z[0, l + 1] = yt * inv
        return 1.0 + k * (1.0 - r), va[l, 0, TOP:TOP + OY, :] + r * yt

    e, yt = lax.fori_loop(0, LO - 1, up, (jnp.ones((OY, LN), F32), va[LO - 1, 0, TOP:TOP + OY, :]))
    top_y[0], top_y[2] = yt, 1.0 / e

    loads[10].wait()
    loads[11].wait()

    def air_up(i, carry):
        e, y = carry
        l = LA - 2 - i
        k = ak_v[l + 1]
        inv = 1.0 / (e + k)
        r = k * inv
        air_r[l + 1] = r
        air_z[l + 1] = y * inv
        return 1.0 + k * (1.0 - r), at_v[l] + r * y

    ea, ya = lax.fori_loop(0, LA - 1, air_up, (jnp.ones((AY, LN), F32), at_v[LA - 1]))
    inv_a = 1.0 / (ea + ak_v[0])
    air_z[0] = ya
    air_r[0] = inv_a

    xt0 = (top_y[0] + sea * top_y[3]) * top_y[2]
    lift([sea * xt0, sea])
    send_terms(1)

    lax.fori_loop(0, LO // GROUP, lambda i, carry, f=substep: f(i, carry, tracers=(1,)), 0)

    def up_second(i, ys):
        l = LO - 2 - i
        elim_z[1, l + 1] = ys * elim_i[l + 1]
        return va[l, 1, TOP:TOP + OY, :] + elim_r[l + 1] * ys

    ys = lax.fori_loop(0, LO - 1, up_second, va[LO - 1, 1, TOP:TOP + OY, :])
    xs0 = (ys + sea * top_y[4]) * top_y[2]

    x_out[0] = xt0
    x_out[LO] = xs0

    def down(l, carry):
        a, b = carry
        r = elim_r[l]
        a = elim_z[0, l] + r * a
        b = elim_z[1, l] + r * b
        x_out[l] = a
        x_out[LO + l] = b
        return a, b

    lax.fori_loop(1, LO, down, (xt0, xs0))
    store = pltpu.make_async_copy(x_out, out_tr, out_sem)
    store.start()

    late = gather(0)
    fields = gather(1) + late
    for f in range(NF):
        out_sf[f] = fields[f]
    ground = at_v[0] * (1.0 - fields[1]) + fields[0]
    x = (air_z[0] + ak_v[0] * ground) * air_r[0]
    out_air[0] = x
    for l in range(1, LA):
        x = air_z[l] + air_r[l] * x
        out_air[l] = x

    for k in range(3):
        exchange_wait(k, gx, DEV - 1).wait_send()
    store.wait()


def hand_on(tr, air, sf, out_tr, out_air, out_sf, tr_v, air_v, sf_v, sem_in, sem_out):
    step = PL // PARTS
    parts = [pl.ds(i * step, step) for i in range(PARTS)]
    trios = [(tr.at[p], tr_v.at[p], out_tr.at[p]) for p in parts] + [(air, air_v, out_air), (sf, sf_v, out_sf)]
    ins = [pltpu.make_async_copy(a, b, sem_in.at[i]) for i, (a, b, _) in enumerate(trios)]
    outs = [pltpu.make_async_copy(b, c, sem_out.at[i]) for i, (_, b, c) in enumerate(trios)]
    for copy in ins:
        copy.start()
    for copy, back in zip(ins, outs):
        copy.wait()
        back.start()
    for back in outs:
        back.wait()


def shards(
    tracers, east_flow, north_flow, ocean_kappa, land_sea, air_temp, air_kappa, air_fluxes,
    weight_tiles, tile_index, send_blocks, receive_blocks,
):
    anyspace = pl.BlockSpec(memory_space=pl.ANY)
    vm = pl.BlockSpec(memory_space=pltpu.VMEM)
    V = pltpu.VMEM
    scratch = [
        V((LO, 2, 64, LN), F32), V((LO, 2, 64, LN), F32), V((PL * OY, 256), BF16), V((512, 256), BF16),
        V((256, LN), BF16), V((LO, OY, LN), F32), V((LO, OY, LN), F32), V((LO - 1, OY, LN), F32),
        V((OY, LN), jnp.int32), V((64, LN), F32), V((LA, AY, LN), F32), V((LA, AY, LN), F32), V((NF, AY, LN), F32),
        V((64, 1024), F32), V((CAP, DEV), jnp.int32), V((CAP, DEV), jnp.int32), V((CAP, DEV), jnp.int32),
        V((3, 16, LN), F32), V((1024, LN), F32), V((2, 1024, LN), BF16),
        V((16, LN, LN), BF16), V((16, 256, LN), BF16), V((16, LN, 256), BF16),
        V((CHUNKS, LN, LN), BF16),
        V((CHUNKS, 1024, CW), F32), V((CHUNKS, 1024, CW), F32),
        V((DEV, 16, LN), F32), V((DEV, 16, LN), F32), V((2, DEV, 8, LN), F32), V((2, DEV, 8, LN), F32),
        V((2 * UNROLL, NF, B, LN), F32), V((256, 256), F32), V((LN, 256), BF16),
        V((ADV, 2, 96, LN), F32), V((ADV, 2, 96, LN), F32), V((ADV, 2, OY, LN), F32), V((ADV, 2, 2, OY, LN), F32),
        V((LO, OY, LN), F32), V((LO, OY, LN), F32), V((LO, OY, LN), F32), V((LO, OY, LN), F32), V((LO, OY, LN), F32),
        V((LO, OY, LN), F32), V((LO, OY, LN), F32), V((2, LO, OY, LN), F32), V((5, OY, LN), F32), V((LA, AY, LN), F32), V((LA, AY, LN), F32),
        V((PL, OY, LN), F32),
        pltpu.SemaphoreType.DMA((13,)), pltpu.SemaphoreType.DMA, pltpu.SemaphoreType.DMA((ADV, 4)),
        pltpu.SemaphoreType.DMA((ADV, 4)), pltpu.SemaphoreType.DMA((3,)), pltpu.SemaphoreType.DMA((3, GX)),
    ]
    out_tr, out_air, out_sf = pl.pallas_call(
        kernel,
        out_shape=(
            jax.ShapeDtypeStruct((PL, OY, LN), F32),
            jax.ShapeDtypeStruct((LA, AY, LN), F32),
            jax.ShapeDtypeStruct((NF, AY, LN), F32),
        ),
        in_specs=[anyspace] * 12,
        out_specs=(anyspace, vm, vm),
        scratch_shapes=scratch,
        compiler_params=pltpu.CompilerParams(
            collective_id=0, has_side_effects=True, vmem_limit_bytes=60 * 1024 * 1024),
        name="coupling_step",
    )(
        tracers, east_flow, north_flow, ocean_kappa, land_sea, air_temp, air_kappa, air_fluxes,
        weight_tiles, *(jnp.swapaxes(x, 1, 2) for x in (tile_index, send_blocks, receive_blocks)),
    )
    out_tr, out_air, out_sf = pl.pallas_call(
        hand_on,
        out_shape=(
            jax.ShapeDtypeStruct((PL, OY, LN), F32),
            jax.ShapeDtypeStruct((LA, AY, LN), F32),
            jax.ShapeDtypeStruct((NF, AY, LN), F32),
        ),
        in_specs=[anyspace] * 3,
        out_specs=[anyspace] * 3,
        scratch_shapes=[
            V((PL, OY, LN), F32), V((LA, AY, LN), F32), V((NF, AY, LN), F32),
            pltpu.SemaphoreType.DMA((PARTS + 2,)), pltpu.SemaphoreType.DMA((PARTS + 2,)),
        ],
        compiler_params=pltpu.CompilerParams(vmem_limit_bytes=60 * 1024 * 1024),
        name="hand_on",
    )(out_tr, out_air, out_sf)
    return out_tr.reshape(2, LO, OY, LN), out_air, out_sf


def solution(mesh):
    return jax.shard_map(
        shards,
        mesh=mesh,
        in_specs=(
            P(None, None, "gy", "gx"),
            P(None, "gy", "gx"),
            P(None, "gy", "gx"),
            P(None, "gy", "gx"),
            P("gy", "gx"),
            P(None, "gy", "gx"),
            P(None, "gy", "gx"),
            P(None, "gy", "gx"),
            P(("gx", "gy"), None, None),
            P(("gx", "gy"), None, None),
            P(("gx", "gy"), None, None),
            P(("gx", "gy"), None, None),
        ),
        out_specs=(P(None, None, "gy", "gx"), P(None, "gy", "gx"), P(None, "gy", "gx")),
        check_vma=False,
    )
```
